512 devices in a mesh: dom: 64 (over y, x, core), slab: 8 (over z).
Axes of the slice: x: 4, y: 8, z: 8, core: 2. Of those that a mesh axis runs over, the one named last changes fastest.
Arguments:
- reference_volume: bfloat16 [4096, 128], P('slab'), may hold values from -6 to 6
- cell_index: int32 [128, 3, 64], P('dom'), may hold values from 0 to 4031
- cell_frac: float32 [128, 3, 64], P('dom'), may hold values from 0 to 1
- warp: bfloat16 [4, 128, 3], P(None, 'dom'), may hold values from 0.5 to 2
- series: int32 [16384], P('dom'), may hold values from 0 to 127, as said below
- position: float32 [16384], P('dom'), may hold values from 0 to 1
- images: bfloat16 [16384, 3, 64, 128], P('dom', None, 'slab'), may hold values from -6 to 6
Outputs:
- residual: bfloat16 [16384, 3, 64, 128], P('dom', None, 'slab')
- warp_grad: float32 [4, 128, 3], P(None, 'dom')
- back_volume: float32 [4096, 128], P('slab')
The draws below stay inside these ranges and needn't reach their ends.
Inputs may be any that keep to these rules, and one draw needn't show every extreme that they name: Every series has at least one particle; series differ in their expected share of particles by up to three-fold.
All inputs are finite; a program needn't handle non-finite values.
Results may differ from the reference program's by a relative error of at most 0.0055.
Values may be sent and summed in bfloat16 or wider, within the bound.
A program may use at most 64 MiB of HBM per device.

```python
import math
import jax
import jax.numpy as jnp
from jax import lax

BOX = 64
TILTS = 3
CTRL = 4
P_DEV = 256
NS = 128
NP = 16384
CELLS = 4096
COLS = 128
N_DOM = 64


def draw_series(key, part):
    key = jax.random.fold_in(key, 11)
    weight_key, pick_key, order_key = jax.random.split(key, 3)
    weights = 1 + jax.random.randint(weight_key, (NS,), 0, 3, dtype=jnp.int32)
    bounds = jnp.cumsum(weights).astype(jnp.int32)
    draws = jax.random.randint(pick_key, (NP,), 0, bounds[NS - 1], dtype=jnp.int32)
    picked = jnp.searchsorted(bounds, draws, side='right').astype(jnp.int32)
    ranks = jax.random.permutation(order_key, NP).astype(jnp.int32)
    return jnp.where(ranks < NS, ranks, picked).astype(jnp.int32)


def set_ends(array, own_key, low, top_value):
    shape = array.shape
    place = [jax.random.randint(jax.random.fold_in(own_key, axis), (), 0, shape[axis]) for axis in range(len(shape))]
    array = array.at[tuple(place)].set(low)
    longest = shape.index(max(shape))
    place[longest] = (place[longest] + 1) % shape[longest]
    return array.at[tuple(place)].set(top_value)


def block_levels(rng, shape, cuts, smallest, top_value):
    gain, own = 1.0, jax.random.fold_in(rng, 6)
    for dim, shards_of in cuts:
        steps = jnp.exp(jax.random.uniform(jax.random.fold_in(own, dim), (shards_of,), jnp.float32, smallest / len(cuts), top_value / len(cuts)))
        gain = gain * jnp.repeat(steps, shape[dim] // shards_of).reshape([-1 if axis == dim else 1 for axis in range(len(shape))])
    return gain


def gaussian(own_key, dims, spread, reach, cuts=(), kind=jnp.bfloat16):
    drawn = jax.random.normal(own_key, dims, jnp.float32) * spread
    if len(cuts) > 0:
        drawn = block_levels(own_key, dims, cuts, -0.22, 0.18) * drawn
    return jnp.clip(drawn, min=-reach, max=reach).astype(kind)


def setup_inputs(seed: int = 0) -> dict:
    key_list = jax.random.split(jax.random.key(seed), 8)
    return {
        "reference_volume": gaussian(key_list[0], (CELLS, COLS), 1.0, 6.0, ((0, 8),)),
        "cell_index": set_ends(jax.random.randint(key_list[1], (NS, TILTS, BOX), 0, CELLS - BOX), jax.random.fold_in(key_list[1], 1), 0, (CELLS - BOX) - 1).astype(jnp.int32),
        "cell_frac": jnp.clip(1.0 * jax.random.uniform(key_list[2], (NS, TILTS, BOX), jnp.float32) ** block_levels(key_list[2], (NS, TILTS, BOX), ((0, 64),), -0.2, 0.2), 0.0, 1.0),
        "warp": jnp.clip(jnp.exp(math.log(2.0) - 1.3862944 * jax.random.uniform(key_list[3], (CTRL, NS, TILTS), jnp.float32) ** block_levels(key_list[3], (CTRL, NS, TILTS), ((1, 64),), -0.2, 0.2)), 0.5, 2.0).astype(jnp.bfloat16),
        "series": draw_series(jax.random.fold_in(key_list[7], 71), 0),
        "position": jnp.clip(1.0 * jax.random.uniform(key_list[5], (NP,), jnp.float32) ** block_levels(key_list[5], (NP,), ((0, 64),), -0.2, 0.2), 0.0, 1.0),
        "images": gaussian(key_list[6], (NP, TILTS, BOX, COLS), 1.0, 6.0, ((0, 64), (2, 8))),
    }


HIGHEST_MODE = lax.Precision.HIGHEST


def bspline_basis(location):
    remain = 1.0 - location
    square = location * location
    cubed = square * location
    return jnp.stack([remain * remain * remain / 6.0, (3.0 * cubed - 6.0 * square + 4.0) / 6.0, (-3.0 * cubed + 3.0 * square + 3.0 * location + 1.0) / 6.0, cubed / 6.0], axis=1)


def reference(reference_volume, cell_index, cell_frac, warp, series, position, images):
    volume = reference_volume.astype(jnp.float32)
    fraction = cell_frac[..., None]
    projection = ((1.0 - fraction) * volume[cell_index] + fraction * volume[cell_index + BOX]).astype(jnp.bfloat16)
    spline_basis = bspline_basis(position)

    def group_step(totals, group_data):
        back_sum, warp_sum = totals
        members, basis_block, images_block = group_data
        predicted = projection[members].astype(jnp.float32)
        chosen = jnp.transpose(warp[:, members, :].astype(jnp.float32), (1, 2, 0))
        tilt_scale = jnp.einsum("pc,ptc->pt", basis_block, chosen, precision=HIGHEST_MODE)
        residual = (images_block.astype(jnp.float32) - tilt_scale[:, :, None, None] * predicted).astype(jnp.bfloat16)
        rounded = lax.optimization_barrier(residual).astype(jnp.float32)
        inner_sum = jnp.sum(rounded * predicted, axis=(2, 3))
        back_sum = back_sum + jax.ops.segment_sum(tilt_scale[:, :, None, None] * rounded, members, num_segments=NS)
        warp_sum = warp_sum + jax.ops.segment_sum(basis_block[:, :, None] * inner_sum[:, None, :], members, num_segments=NS)
        return (back_sum, warp_sum), residual

    initial = (jnp.zeros((NS, TILTS, BOX, COLS), jnp.float32), jnp.zeros((NS, CTRL, TILTS), jnp.float32))
    blocks = (series.reshape(N_DOM, P_DEV), spline_basis.reshape(N_DOM, P_DEV, CTRL), images.reshape(N_DOM, P_DEV, TILTS, BOX, COLS))
    (back_sum, warp_sum), residual = lax.scan(group_step, initial, blocks)
    residual = residual.reshape(NP, TILTS, BOX, COLS)
    warp_grad = jnp.transpose(warp_sum, (1, 0, 2)) * (-1.0 / (BOX * BOX))
    flat_low = cell_index.reshape(-1)
    flat_frac = cell_frac.reshape(-1, 1)
    flat_back = back_sum.reshape(-1, COLS)
    back_volume = jnp.zeros((CELLS, COLS), jnp.float32)
    back_volume = back_volume.at[flat_low].add((1.0 - flat_frac) * flat_back)
    back_volume = back_volume.at[flat_low + BOX].add(flat_frac * flat_back)
    return residual, warp_grad, back_volume
```

```python
import jax
import jax.numpy as jnp
from jax import lax
from jax.experimental import pallas as pl
from jax.experimental.pallas import tpu as pltpu
from jax.sharding import PartitionSpec as P

MESH = pl.DeviceIdType.MESH
F32, BF16 = jnp.float32, jnp.bfloat16
NY, NX, NC, NZ = 8, 4, 2, 8
BOX, TILTS, CTRL, COLS = 64, 3, 4, 128
PARTS = 256
BAND = BOX // NZ
ROWS = TILTS * BAND
OWN = 2
NS = NY * NX * NC * OWN
GROUP = NY * OWN
SLAB = BOX * BOX // NZ
CELLS = BOX * BOX
CPY = COLS // NY

(META_Y, META_X, META_C, PZ, PY, PX, PC, SC, SX, SY, VZ, VC, VX, VY, QC, QX, QY, QZ) = range(18)


def split2(v):
    hi = v.astype(BF16)
    return hi, (v - hi.astype(F32)).astype(BF16)


def split3(v):
    hi = v.astype(BF16)
    rest = v - hi.astype(F32)
    mid = rest.astype(BF16)
    return hi, mid, (rest - mid.astype(F32)).astype(BF16)


def dot(a, b):
    return jnp.dot(a, b, preferred_element_type=F32)


def kernel(
    vol,
    idx,
    frac,
    warp,
    series,
    pos,
    images,
    res_out,
    wg_out,
    back_out,
    imgv,
    xf,
    xt,
    tmp,
    meta,
    psrc,
    prcv,
    pall,
    pgf,
    pf,
    bs,
    brc,
    brx,
    ysrc,
    yrcv,
    wsp,
    zsrc,
    zrcv,
    crcv,
    xrcv,
    vall,
    qsrc,
    qrc,
    qrx,
    qry,
    qrz,
    last,
    rf,
    rb,
    ssem,
    rsem,
    lsem,
):
    d, z = lax.axis_index("dom"), lax.axis_index("slab")
    c, x, y = lax.rem(d, NC), lax.rem(d // NC, NX), d // (NC * NX)

    def spot(axis, k):
        at = {"y": y, "x": x, "c": c, "z": z}
        size = {"y": NY, "x": NX, "c": NC, "z": NZ}[axis]
        at[axis] = lax.rem(at[axis] + k, size)
        return ((at["y"] * NX + at["x"]) * NC + at["c"], at["z"]), at[axis]

    def send(row, axis, src, dst):
        size = {"y": NY, "x": NX, "c": NC, "z": NZ}[axis]
        copies = []
        for k in range(1, size):
            device, there = spot(axis, k)
            copy = pltpu.make_async_remote_copy(
                src_ref=src(there),
                dst_ref=dst,
                send_sem=ssem.at[row, k],
                recv_sem=rsem.at[row, k],
                device_id=device,
                device_id_type=MESH,
            )
            copy.start()
            copies.append(copy)
        return copies

    def arrive(copies):
        for copy in copies:
            copy.wait_recv()

    sent = []

    barrier = pltpu.get_barrier_semaphore()
    for axis, size in (("y", NY), ("x", NX), ("c", NC), ("z", NZ)):
        for k in range(1, size):
            pl.semaphore_signal(barrier, inc=1, device_id=spot(axis, k)[0], device_id_type=MESH)

    image_copy = pltpu.make_async_copy(images, imgv, lsem.at[0])
    image_copy.start()

    lane8 = lax.broadcasted_iota(jnp.int32, (8, COLS), 1)
    tmp[...] = jnp.zeros_like(tmp)
    for q in range(OWN):
        tmp[0, q * 4 : q * 4 + 3, 0:BOX] = idx[q].astype(F32)
        tmp[1, q * 4 : q * 4 + 3, 0:BOX] = frac[q]
    for k in range(CTRL):
        one = warp[k].astype(F32)
        for q in range(OWN):
            tmp[2, q * 4 + k : q * 4 + k + 1, 0:TILTS] = one[q : q + 1]
    own_idx, own_frac, own_warp = tmp[0], tmp[1], tmp[2]
    band_idx = pltpu.roll(own_idx, lax.rem(COLS - z * BAND, COLS), 1)
    band_frac = pltpu.roll(own_frac, lax.rem(COLS - z * BAND + BAND, COLS), 1)
    rolled_warp = pltpu.roll(own_warp, 2 * BAND, 1)
    meta[c, x, y] = jnp.where(
        lane8 < BAND, band_idx, jnp.where(lane8 < 2 * BAND, band_frac, rolled_warp)
    )

    columns = jnp.transpose(jnp.where(lane8 < BOX, own_idx, pltpu.roll(own_frac, BOX, 1)))
    cell = (lax.broadcasted_iota(jnp.int32, (BOX, SLAB), 1) + z * SLAB).astype(F32)
    volume = vol[...]
    for q in range(OWN):
        for t in range(TILTS):
            low = columns[0:BOX, q * 4 + t : q * 4 + t + 1]
            part = columns[BOX : 2 * BOX, q * 4 + t : q * 4 + t + 1]
            weight = jnp.where(cell == low, 1.0 - part, 0.0) + jnp.where(cell == low + BOX, part, 0.0)
            hi, mid, lo = split3(weight)
            value = dot(hi, volume) + (dot(mid, volume) + dot(lo, volume))
            psrc[q * TILTS + t] = value.reshape(NZ, BAND, COLS)

    pl.semaphore_wait(barrier, NY + NX + NC + NZ - 4)
    meta_y = send(META_Y, "y", lambda there: meta.at[c, x, y], meta.at[c, x, y])
    p_z = send(PZ, "z", lambda there: psrc.at[:, there], prcv.at[z])
    sent += meta_y + p_z

    image_copy.wait()

    def widen(i, _):
        part = imgv[pl.ds(i * 32, 32)].astype(F32)
        xf[pl.ds(pl.multiple_of(i * 32 * ROWS, 32 * ROWS), 32 * ROWS), :] = part.reshape(32 * ROWS, COLS)
        return 0

    lax.fori_loop(0, PARTS // 32, widen, 0)

    def gather_rows(r, _):
        xt[r] = xf[pl.ds(r, PARTS, stride=ROWS), :].astype(BF16)
        return 0

    lax.fori_loop(0, ROWS, gather_rows, 0)

    arrive(meta_y)
    meta_x = send(META_X, "x", lambda there: meta.at[c, x], meta.at[c, x])
    sent += meta_x

    row = lax.broadcasted_iota(jnp.int32, (NS, PARTS), 0)
    name = (
        lax.rem(row, GROUP) // OWN * (NX * NC * OWN)
        + lax.rem(row // GROUP, NX) * (NC * OWN)
        + row // (GROUP * NX) * OWN
        + lax.rem(row, OWN)
    )
    hit = series[...].reshape(1, PARTS) == name
    hot = hit.astype(F32)
    hot16 = hot.astype(BF16)
    at = pos[...].reshape(1, PARTS)
    remain = 1.0 - at
    square = at * at
    cubed = square * at
    basis = [
        remain * remain * remain / 6.0,
        (3.0 * cubed - 6.0 * square + 4.0) / 6.0,
        (-3.0 * cubed + 3.0 * square + 3.0 * at + 1.0) / 6.0,
        cubed / 6.0,
    ]

    arrive(p_z)
    own = psrc[:, z]
    for k in range(1, NZ):
        own = own + prcv[lax.rem(z + k, NZ)]
    pall[c, x, y] = own.reshape(OWN * ROWS, COLS).astype(BF16)
    p_y = send(PY, "y", lambda there: pall.at[c, x, y], pall.at[c, x, y])
    sent += p_y

    arrive(meta_x)
    meta_c = send(META_C, "c", lambda there: meta.at[c], meta.at[c])
    sent += meta_c
    arrive(meta_c)

    flat_meta = meta.reshape(NS * 4, COLS)
    lane = lax.broadcasted_iota(jnp.int32, (NS, COLS), 1)
    table = jnp.zeros((NS, COLS), F32)
    for k in range(CTRL):
        rows = pltpu.roll(flat_meta[pl.ds(k, NS, stride=4), :], COLS - 2 * BAND + 3 * k, 1)
        table = jnp.where((lane >= 3 * k) & (lane < 3 * k + 3), rows, table)
    chosen = dot(jnp.transpose(table)[0:16].astype(BF16), hot16)
    scale = [
        sum(basis[k] * chosen[3 * k + t : 3 * k + t + 1] for k in range(CTRL)) for t in range(TILTS)
    ]

    squares = jnp.zeros((NS, COLS), F32)
    for t in range(TILTS):
        weight = jnp.where(hit, scale[t], 0.0)
        squares = jnp.where(lane == t, jnp.sum(weight * weight, axis=1, keepdims=True), squares)
        both = jnp.concatenate(split2(weight), axis=0)
        for u in range(0, BAND, 2):
            r = t * BAND + u
            pair = dot(both, jnp.concatenate([xt[r], xt[r + 1]], axis=1))
            pair = pair[:NS] + pair[NS:]
            bs[:, r] = pair[:, :COLS].reshape(NC * NX, GROUP, COLS)
            bs[:, r + 1] = pair[:, COLS:].reshape(NC * NX, GROUP, COLS)
    bs[:, ROWS] = squares.reshape(NC * NX, GROUP, COLS)

    other, there = spot("c", 1)
    c_copies = []
    for k in range(NX):
        to = lax.rem(x + 1 + k, NX)
        copy = pltpu.make_async_remote_copy(
            src_ref=bs.at[there * NX + to],
            dst_ref=brc.at[to],
            send_sem=ssem.at[SC, k],
            recv_sem=rsem.at[SC, k],
            device_id=other,
            device_id_type=MESH,
        )
        copy.start()
        c_copies.append(copy)
    sent += c_copies
    x_copies = []
    for k in range(NX):
        to = lax.rem(x + 1 + k, NX)
        c_copies[k].wait_recv()
        brc[to] = brc[to] + bs[c * NX + to]
        if k < NX - 1:
            copy = pltpu.make_async_remote_copy(
                src_ref=brc.at[to],
                dst_ref=brx.at[x],
                send_sem=ssem.at[SX, k + 1],
                recv_sem=rsem.at[SX, k + 1],
                device_id=spot("x", k + 1)[0],
                device_id_type=MESH,
            )
            copy.start()
            x_copies.append(copy)
    sent += x_copies

    flat_group = meta.at[c, x].reshape(NY * 8, COLS)
    cells = lax.broadcasted_iota(jnp.int32, (GROUP, CELLS), 1).astype(F32)
    for t in range(TILTS):
        group = flat_group[pl.ds(t, GROUP, stride=4), :]
        for u in range(BAND):
            low = group[:, u : u + 1]
            part = group[:, BAND + u : BAND + u + 1]
            weight = jnp.where(
                cells == low, 1.0 - part, jnp.where(cells == low + BOX, part, 0.0)
            )
            wsp[(t * BAND + u) * GROUP : (t * BAND + u + 1) * GROUP, :] = weight.astype(BF16)

    arrive(p_y)
    pgf[...] = pall[c, x].reshape(GROUP * ROWS, COLS).astype(F32)

    arrive(x_copies)
    total = brc[x]
    for k in range(1, NX):
        total = total + brx[lax.rem(x + k, NX)]
    squares = total[ROWS]
    fixed = []
    for t in range(TILTS):
        for u in range(BAND):
            r = t * BAND + u
            fixed.append(total[r] - squares[:, t : t + 1] * pgf[pl.ds(r, GROUP, stride=ROWS), :])
    turned = jnp.transpose(jnp.concatenate(fixed, axis=0))
    ysrc[...] = turned.reshape(NY, CPY, ROWS * GROUP).astype(BF16)
    s_y = send(SY, "y", lambda there: ysrc.at[there], yrcv.at[y])
    p_x = send(PX, "x", lambda there: pall.at[c, x], pall.at[c, x])
    sent += s_y + p_x

    arrive(s_y)
    total = ysrc[y].astype(F32)
    for k in range(1, NY):
        total = total + yrcv[lax.rem(y + k, NY)].astype(F32)
    both = jnp.concatenate(split2(total), axis=0)
    for k in range(NZ):
        part = dot(both, wsp[:, k * SLAB : (k + 1) * SLAB])
        zsrc[k] = (part[:CPY] + part[CPY:]).astype(BF16)
    v_z = send(VZ, "z", lambda there: zsrc.at[there], zrcv.at[z])
    sent += v_z

    arrive(p_x)
    p_c = send(PC, "c", lambda there: pall.at[c], pall.at[c])
    sent += p_c
    arrive(p_c)
    pf[...] = pall[...].reshape(NS * ROWS, COLS).astype(F32)
    hot_turned = jnp.transpose(hot).astype(BF16)
    lane_p = lax.broadcasted_iota(jnp.int32, (PARTS, COLS), 1)
    turned = jnp.transpose(jnp.concatenate(scale + basis + [basis[0]], axis=0))
    inner = jnp.zeros((PARTS, COLS), F32)
    for t in range(TILTS):
        scale_column = turned[:, t : t + 1]

        def one_row(u, acc):
            r = t * BAND + u
            guess = dot(hot_turned, pf[pl.ds(r, NS, stride=ROWS), :].astype(BF16))
            left = (xt[r].astype(F32) - scale_column * guess).astype(BF16).astype(F32)
            rf[pl.ds(r, PARTS, stride=ROWS), :] = left
            return acc + left * guess

        acc = lax.fori_loop(0, BAND, one_row, jnp.zeros((PARTS, COLS), F32))
        inner = jnp.where(lax.rem(lane_p, TILTS) == t, jnp.sum(acc, axis=1, keepdims=True), inner)

    def narrow(i, _):
        part = rf[pl.ds(pl.multiple_of(i * 32 * ROWS, 32 * ROWS), 32 * ROWS), :]
        rb[pl.ds(i * 32, 32)] = part.reshape(32, TILTS, BAND, COLS).astype(BF16)
        return 0

    lax.fori_loop(0, PARTS // 32, narrow, 0)
    res_copy = pltpu.make_async_copy(rb, res_out, lsem.at[1])
    res_copy.start()
    term = jnp.zeros((PARTS, COLS), F32)
    for k in range(CTRL):
        term = jnp.where(lane_p // TILTS == k, turned[:, TILTS + k : TILTS + k + 1] * inner, term)
    hi, mid, lo = split3(term)
    grad = (dot(hot16, hi) + (dot(hot16, mid) + dot(hot16, lo))) * (-1.0 / (BOX * BOX))
    qsrc[...] = grad.reshape(NC, NX, GROUP, COLS)
    q_c = send(QC, "c", lambda there: qsrc.at[there], qrc)
    sent += q_c

    arrive(v_z)
    total = zsrc[z].astype(F32)
    for k in range(1, NZ):
        total = total + zrcv[lax.rem(z + k, NZ)].astype(F32)
    crcv[c] = total
    v_c = send(VC, "c", lambda there: crcv.at[c], crcv.at[c])
    sent += v_c
    arrive(q_c)
    qrc[...] = qrc[...] + qsrc[c]
    q_x = send(QX, "x", lambda there: qrc.at[there], qrx.at[x])
    sent += q_x
    arrive(v_c)
    xrcv[x] = crcv[0] + crcv[1]
    v_x = send(VX, "x", lambda there: xrcv.at[x], xrcv.at[x])
    sent += v_x
    arrive(q_x)
    total = qrc[x]
    for k in range(1, NX):
        total = total + qrx[lax.rem(x + k, NX)]
    qry[y] = total
    q_y = send(QY, "y", lambda there: qry.at[y], qry.at[y])
    sent += q_y
    arrive(v_x)
    vall[y] = ((xrcv[0] + xrcv[1]) + (xrcv[2] + xrcv[3])).astype(BF16)
    v_y = send(VY, "y", lambda there: vall.at[y], vall.at[y])
    sent += v_y
    arrive(q_y)
    total = qry[0]
    for k in range(1, NY):
        total = total + qry[k]
    qrz[z] = total
    q_z = send(QZ, "z", lambda there: qrz.at[z], qrz.at[z])
    sent += q_z
    arrive(v_y)
    back_out[...] = jnp.transpose(vall[...].astype(F32).reshape(COLS, SLAB))
    arrive(q_z)
    total = qrz[0]
    for k in range(1, NZ):
        total = total + qrz[k]
    last[...] = total
    mine = last[pl.ds(y * OWN, OWN), :]
    for k in range(CTRL):
        wg_out[k] = pltpu.roll(mine, (COLS - TILTS * k) % COLS, 1)[:, 0:TILTS]
    res_copy.wait()
    for copy in sent:
        copy.wait_send()


def shards(reference_volume, cell_index, cell_frac, warp, series, position, images):
    vmem = pl.BlockSpec(memory_space=pltpu.VMEM)
    hbm = pl.BlockSpec(memory_space=pl.ANY)
    scratch = [
        pltpu.VMEM((PARTS, TILTS, BAND, COLS), BF16),
        pltpu.VMEM((PARTS * ROWS, COLS), F32),
        pltpu.VMEM((ROWS, PARTS, COLS), BF16),
        pltpu.VMEM((3, 8, COLS), F32),
        pltpu.VMEM((NC, NX, NY, 8, COLS), F32),
        pltpu.VMEM((OWN * TILTS, NZ, BAND, COLS), F32),
        pltpu.VMEM((NZ, OWN * TILTS, BAND, COLS), F32),
        pltpu.VMEM((NC, NX, NY, OWN * ROWS, COLS), BF16),
        pltpu.VMEM((GROUP * ROWS, COLS), F32),
        pltpu.VMEM((NS * ROWS, COLS), F32),
        pltpu.VMEM((NC * NX, ROWS + 1, GROUP, COLS), F32),
        pltpu.VMEM((NX, ROWS + 1, GROUP, COLS), F32),
        pltpu.VMEM((NX, ROWS + 1, GROUP, COLS), F32),
        pltpu.VMEM((NY, CPY, ROWS * GROUP), BF16),
        pltpu.VMEM((NY, CPY, ROWS * GROUP), BF16),
        pltpu.VMEM((ROWS * GROUP, CELLS), BF16),
        pltpu.VMEM((NZ, CPY, SLAB), BF16),
        pltpu.VMEM((NZ, CPY, SLAB), BF16),
        pltpu.VMEM((NC, CPY, SLAB), F32),
        pltpu.VMEM((NX, CPY, SLAB), F32),
        pltpu.VMEM((NY, CPY, SLAB), BF16),
        pltpu.VMEM((NC, NX, GROUP, COLS), F32),
        pltpu.VMEM((NX, GROUP, COLS), F32),
        pltpu.VMEM((NX, GROUP, COLS), F32),
        pltpu.VMEM((NY, GROUP, COLS), F32),
        pltpu.VMEM((NZ, GROUP, COLS), F32),
        pltpu.VMEM((GROUP, COLS), F32),
        pltpu.VMEM((PARTS * ROWS, COLS), F32),
        pltpu.VMEM((PARTS, TILTS, BAND, COLS), BF16),
        pltpu.SemaphoreType.DMA((18, 8)),
        pltpu.SemaphoreType.DMA((18, 8)),
        pltpu.SemaphoreType.DMA((2,)),
    ]
    return pl.pallas_call(
        kernel,
        out_shape=(
            jax.ShapeDtypeStruct((PARTS, TILTS, BAND, COLS), BF16),
            jax.ShapeDtypeStruct((CTRL, OWN, TILTS), F32),
            jax.ShapeDtypeStruct((SLAB, COLS), F32),
        ),
        in_specs=[vmem] * 6 + [hbm],
        out_specs=(hbm, vmem, vmem),
        scratch_shapes=scratch,
        compiler_params=pltpu.CompilerParams(
            collective_id=0, has_side_effects=True, vmem_limit_bytes=56 << 20
        ),
        name="refine",
    )(reference_volume, cell_index, cell_frac, warp, series, position, images)


def solution(mesh):
    placed = (
        P("slab", None),
        P("dom", None, None),
        P("dom", None, None),
        P(None, "dom", None),
        P("dom"),
        P("dom"),
        P("dom", None, "slab", None),
    )
    return jax.shard_map(
        shards,
        mesh=mesh,
        in_specs=placed,
        out_specs=(P("dom", None, "slab", None), P(None, "dom", None), P("slab", None)),
        check_vma=False,
    )
```

```python
import jax
import jax.numpy as jnp
from jax import lax
from jax.experimental import pallas as pl
from jax.experimental.pallas import tpu as pltpu
from jax.sharding import PartitionSpec as P

MESH = pl.DeviceIdType.MESH
F32, BF16 = jnp.float32, jnp.bfloat16
NY, NX, NC, NZ = 8, 4, 2, 8
BOX, TILTS, CTRL, COLS = 64, 3, 4, 128
PARTS = 256
BAND = BOX // NZ
ROWS = TILTS * BAND
OWN = 2
NS = NY * NX * NC * OWN
GROUP = NY * OWN
SLAB = BOX * BOX // NZ
CELLS = BOX * BOX
CPY = COLS // NY

(META_Y, META_X, META_C, PZ, PY, PX, PC, SC, SX, SY, VZ, VC, VX, VY, QC, QX, QY, QZ) = range(18)
LAST = QZ


def split2(v):
    hi = v.astype(BF16)
    return hi, (v - hi.astype(F32)).astype(BF16)


def split3(v):
    hi = v.astype(BF16)
    rest = v - hi.astype(F32)
    mid = rest.astype(BF16)
    return hi, mid, (rest - mid.astype(F32)).astype(BF16)


def dot(a, b):
    return jnp.dot(a, b, preferred_element_type=F32)


def kernel(
    vol_in,
    idx_in,
    frac_in,
    warp_in,
    series_in,
    pos_in,
    images,
    res_out,
    wg_out,
    back_out,
    vol,
    idx,
    frac,
    warp,
    series,
    pos,
    imgv,
    xf,
    xt,
    tmp,
    meta,
    psrc,
    prcv,
    pall,
    pgf,
    pf,
    bs,
    brc,
    brx,
    ysrc,
    yrcv,
    wsp,
    zsrc,
    zrcv,
    crcv,
    xrcv,
    vall,
    qsrc,
    qrc,
    qrx,
    qry,
    qrz,
    last,
    rf,
    rb,
    ssem,
    rsem,
    lsem,
):
    d, z = lax.axis_index("dom"), lax.axis_index("slab")
    c, x, y = lax.rem(d, NC), lax.rem(d // NC, NX), d // (NC * NX)

    def spot(axis, k):
        at = {"y": y, "x": x, "c": c, "z": z}
        size = {"y": NY, "x": NX, "c": NC, "z": NZ}[axis]
        at[axis] = lax.rem(at[axis] + k, size)
        return ((at["y"] * NX + at["x"]) * NC + at["c"], at["z"]), at[axis]

    def remote(row, device, src, dst):
        return pltpu.make_async_remote_copy(
            src_ref=src,
            dst_ref=dst,
            send_sem=ssem.at[row],
            recv_sem=rsem.at[row],
            device_id=device,
            device_id_type=MESH,
        )

    def send(row, axis, src, dst, bulk):
        size = {"y": NY, "x": NX, "c": NC, "z": NZ}[axis]
        for k in range(1, size):
            device, there = spot(axis, k)
            remote(row, device, src(there), dst).start()
        whole = remote(row, spot(axis, 1)[0], bulk, bulk)
        sent.append(whole)
        return whole

    sent = []

    barrier = pltpu.get_barrier_semaphore()
    for axis, size in (("y", NY), ("x", NX), ("c", NC), ("z", NZ)):
        for k in range(1, size):
            pl.semaphore_signal(barrier, inc=1, device_id=spot(axis, k)[0], device_id_type=MESH)

    small_copies = [
        pltpu.make_async_copy(a, b, lsem.at[k])
        for k, (a, b) in enumerate(
            (
                (idx_in, idx),
                (frac_in, frac),
                (warp_in, warp),
                (vol_in, vol),
                (series_in, series),
                (pos_in, pos),
            )
        )
    ]
    for copy in small_copies:
        copy.start()
    step = PARTS // 8
    for k in range(8):
        rows = pl.ds(k * step, step)
        pltpu.make_async_copy(images.at[rows], imgv.at[rows], lsem.at[6]).start()

    lane8 = lax.broadcasted_iota(jnp.int32, (8, COLS), 1)
    tmp[...] = jnp.zeros_like(tmp)
    for copy in small_copies[:3]:
        copy.wait()
    for q in range(OWN):
        for t in range(TILTS):
            at = q * 4 + t
            tmp[0, at : at + 1, 0:BOX] = idx[t, q : q + 1].astype(F32)
            tmp[1, at : at + 1, 0:BOX] = frac[t, q : q + 1]
            tmp[2, at : at + 1, 0:CTRL] = warp[t].astype(F32)[q : q + 1]
    own_idx, own_frac, own_warp = tmp[0], tmp[1], tmp[2]
    band_idx = pltpu.roll(own_idx, lax.rem(COLS - z * BAND, COLS), 1)
    band_frac = pltpu.roll(own_frac, lax.rem(COLS - z * BAND + BAND, COLS), 1)
    rolled_warp = pltpu.roll(own_warp, 2 * BAND, 1)
    meta[c, x, y] = jnp.where(
        lane8 < BAND, band_idx, jnp.where(lane8 < 2 * BAND, band_frac, rolled_warp)
    )

    pl.semaphore_wait(barrier, NY + NX + NC + NZ - 4)
    meta_y = send(META_Y, "y", lambda there: meta.at[c, x, y], meta.at[c, x, y], meta.at[0, 0, 0 : NY - 1])

    columns = jnp.transpose(jnp.where(lane8 < BOX, own_idx, pltpu.roll(own_frac, BOX, 1)))
    cell = (lax.broadcasted_iota(jnp.int32, (BOX, SLAB), 1) + z * SLAB).astype(F32)
    small_copies[3].wait()
    volume = vol[...]
    for q in range(OWN):
        for t in range(TILTS):
            low = columns[0:BOX, q * 4 + t : q * 4 + t + 1]
            part = columns[BOX : 2 * BOX, q * 4 + t : q * 4 + t + 1]
            weight = jnp.where(cell == low, 1.0 - part, 0.0) + jnp.where(cell == low + BOX, part, 0.0)
            hi, mid, lo = split3(weight)
            value = dot(hi, volume) + (dot(mid, volume) + dot(lo, volume))
            psrc[q * TILTS + t] = value.reshape(NZ, BAND, COLS)

    p_z = send(PZ, "z", lambda there: psrc.at[:, there], prcv.at[z], prcv.at[0 : NZ - 1])

    pltpu.make_async_copy(images, imgv, lsem.at[6]).wait()
    for copy in small_copies[4:]:
        copy.wait()

    def widen(i, _):
        part = imgv[pl.ds(i * 32, 32)].astype(F32)
        xf[pl.ds(pl.multiple_of(i * 32 * ROWS, 32 * ROWS), 32 * ROWS), :] = part.reshape(32 * ROWS, COLS)
        return 0

    lax.fori_loop(0, PARTS // 32, widen, 0)

    def gather_rows(r, _):
        xt[r] = xf[pl.ds(r, PARTS, stride=ROWS), :].astype(BF16)
        return 0

    lax.fori_loop(0, ROWS, gather_rows, 0)

    meta_y.wait_recv()
    meta_x = send(META_X, "x", lambda there: meta.at[c, x], meta.at[c, x], meta.at[0, 0 : NX - 1])

    row = lax.broadcasted_iota(jnp.int32, (NS, PARTS), 0)
    name = (
        lax.rem(row, GROUP) // OWN * (NX * NC * OWN)
        + lax.rem(row // GROUP, NX) * (NC * OWN)
        + row // (GROUP * NX) * OWN
        + lax.rem(row, OWN)
    )
    hit = series[...].reshape(1, PARTS) == name
    hot = hit.astype(F32)
    hot16 = hot.astype(BF16)
    at = pos[...].reshape(1, PARTS)
    remain = 1.0 - at
    square = at * at
    cubed = square * at
    basis = [
        remain * remain * remain / 6.0,
        (3.0 * cubed - 6.0 * square + 4.0) / 6.0,
        (-3.0 * cubed + 3.0 * square + 3.0 * at + 1.0) / 6.0,
        cubed / 6.0,
    ]

    p_z.wait_recv()
    own = psrc[:, z]
    for k in range(1, NZ):
        own = own + prcv[lax.rem(z + k, NZ)]
    pall[c, x, y] = own.reshape(OWN * ROWS, COLS).astype(BF16)
    p_y = send(PY, "y", lambda there: pall.at[c, x, y], pall.at[c, x, y], pall.at[0, 0, 0 : NY - 1])

    meta_x.wait_recv()
    meta_c = send(META_C, "c", lambda there: meta.at[c], meta.at[c], meta.at[0])
    meta_c.wait_recv()

    flat_meta = meta.reshape(NS * 4, COLS)
    lane = lax.broadcasted_iota(jnp.int32, (NS, COLS), 1)
    table = jnp.zeros((NS, COLS), F32)
    for t in range(TILTS):
        rows = pltpu.roll(flat_meta[pl.ds(t, NS, stride=4), :], COLS - 2 * BAND + CTRL * t, 1)
        table = jnp.where(lane // CTRL == t, rows, table)
    chosen = dot(jnp.transpose(table)[0:16].astype(BF16), hot16)
    scale = [
        sum(basis[k] * chosen[CTRL * t + k : CTRL * t + k + 1] for k in range(CTRL))
        for t in range(TILTS)
    ]

    squares = jnp.zeros((NS, COLS), F32)
    for t in range(TILTS):
        weight = jnp.where(hit, scale[t], 0.0)
        squares = jnp.where(lane == t, jnp.sum(weight * weight, axis=1, keepdims=True), squares)
        both = jnp.concatenate(split2(weight), axis=0)
        for u in range(0, BAND, 2):
            r = t * BAND + u
            pair = dot(both, jnp.concatenate([xt[r], xt[r + 1]], axis=1))
            pair = pair[:NS] + pair[NS:]
            bs[:, r] = pair[:, :COLS].reshape(NC * NX, GROUP, COLS)
            bs[:, r + 1] = pair[:, COLS:].reshape(NC * NX, GROUP, COLS)
    bs[:, ROWS] = squares.reshape(NC * NX, GROUP, COLS)

    p_y.wait_recv()
    p_x = send(PX, "x", lambda there: pall.at[c, x], pall.at[c, x], pall.at[0, 0 : NX - 1])

    other, there = spot("c", 1)
    c_copies = []
    for k in range(NX):
        to = lax.rem(x + 1 + k, NX)
        row = SC if k == 0 else LAST + k
        c_copies.append(remote(row, other, bs.at[there * NX + to], brc.at[to]))
        c_copies[k].start()
    for k in range(NX):
        to = lax.rem(x + 1 + k, NX)
        c_copies[k].wait_recv()
        brc[to] = brc[to] + bs[c * NX + to]
        if k < NX - 1:
            remote(SX, spot("x", k + 1)[0], brc.at[to], brx.at[x]).start()
    s_x = remote(SX, other, brx.at[0 : NX - 1], brx.at[0 : NX - 1])
    sent += c_copies + [s_x]

    pgf[...] = pall[c, x].reshape(GROUP * ROWS, COLS).astype(F32)

    flat_group = meta.at[c, x].reshape(NY * 8, COLS)
    cells = lax.broadcasted_iota(jnp.int32, (GROUP, CELLS), 1).astype(F32)
    for t in range(TILTS):
        group = flat_group[pl.ds(t, GROUP, stride=4), :]
        for u in range(BAND):
            low = group[:, u : u + 1]
            part = group[:, BAND + u : BAND + u + 1]
            weight = jnp.where(
                cells == low, 1.0 - part, jnp.where(cells == low + BOX, part, 0.0)
            )
            wsp[(t * BAND + u) * GROUP : (t * BAND + u + 1) * GROUP, :] = weight.astype(BF16)

    p_x.wait_recv()
    p_c = send(PC, "c", lambda there: pall.at[c], pall.at[c], pall.at[0])
    hot_turned = jnp.transpose(hot).astype(BF16)
    lane_p = lax.broadcasted_iota(jnp.int32, (PARTS, COLS), 1)
    turned = jnp.transpose(jnp.concatenate(scale + basis + [basis[0]], axis=0))
    inner = jnp.zeros((PARTS, COLS), F32)
    p_c.wait_recv()
    pf[...] = pall[...].reshape(NS * ROWS, COLS).astype(F32)
    for t in range(TILTS):
        scale_column = turned[:, t : t + 1]
        acc = jnp.zeros((PARTS, COLS), F32)
        for u in range(0, BAND, 2):
            r = t * BAND + u
            pair = [pf[pl.ds(r + k, NS, stride=ROWS), :].astype(BF16) for k in range(2)]
            guesses = dot(hot_turned, jnp.concatenate(pair, axis=1))
            for k in range(2):
                guess = guesses[:, k * COLS : (k + 1) * COLS]
                left = (xt[r + k].astype(F32) - scale_column * guess).astype(BF16).astype(F32)
                rf[(r + k) * PARTS : (r + k + 1) * PARTS, :] = left
                acc = acc + left * guess
        inner = jnp.where(lane_p // CTRL == t, jnp.sum(acc, axis=1, keepdims=True), inner)

    def narrow(i, _):
        for k in range(16):
            part = rf[pl.ds(i * 16 + k, ROWS, stride=PARTS), :]
            rb[i * 16 + k] = part.reshape(TILTS, BAND, COLS).astype(BF16)
        return 0

    lax.fori_loop(0, PARTS // 16, narrow, 0)
    for k in range(8):
        rows = pl.ds(k * step, step)
        pltpu.make_async_copy(rb.at[rows], res_out.at[rows], lsem.at[7]).start()
    term = jnp.zeros((PARTS, COLS), F32)
    for k in range(CTRL):
        term = jnp.where(lax.rem(lane_p, CTRL) == k, turned[:, TILTS + k : TILTS + k + 1] * inner, term)
    hi, mid, lo = split3(term)
    grad = (dot(hot16, hi) + (dot(hot16, mid) + dot(hot16, lo))) * (-1.0 / (BOX * BOX))
    qsrc[...] = grad.reshape(NC, NX, GROUP, COLS)
    q_c = send(QC, "c", lambda there: qsrc.at[there], qrc, qrc)

    s_x.wait_recv()
    total = brc[x]
    for k in range(1, NX):
        total = total + brx[lax.rem(x + k, NX)]
    squares = total[ROWS]
    fixed = []
    for t in range(TILTS):
        for u in range(BAND):
            r = t * BAND + u
            fixed.append(total[r] - squares[:, t : t + 1] * pgf[pl.ds(r, GROUP, stride=ROWS), :])
    turned = jnp.transpose(jnp.concatenate(fixed, axis=0))
    ysrc[...] = turned.reshape(NY, CPY, ROWS * GROUP).astype(BF16)
    s_y = send(SY, "y", lambda there: ysrc.at[there], yrcv.at[y], yrcv.at[0 : NY - 1])

    q_c.wait_recv()
    qrc[...] = qrc[...] + qsrc[c]
    q_x = send(QX, "x", lambda there: qrc.at[there], qrx.at[x], qrx.at[0 : NX - 1])
    s_y.wait_recv()
    total = ysrc[y].astype(F32)
    for k in range(1, NY):
        total = total + yrcv[lax.rem(y + k, NY)].astype(F32)
    both = jnp.concatenate(split2(total), axis=0)
    for k in range(NZ):
        part = dot(both, wsp[:, k * SLAB : (k + 1) * SLAB])
        zsrc[k] = (part[:CPY] + part[CPY:]).astype(BF16)
    v_z = send(VZ, "z", lambda there: zsrc.at[there], zrcv.at[z], zrcv.at[0 : NZ - 1])

    q_x.wait_recv()
    total = qrc[x]
    for k in range(1, NX):
        total = total + qrx[lax.rem(x + k, NX)]
    qry[y] = total
    q_y = send(QY, "y", lambda there: qry.at[y], qry.at[y], qry.at[0 : NY - 1])
    v_z.wait_recv()
    total = zsrc[z].astype(F32)
    for k in range(1, NZ):
        total = total + zrcv[lax.rem(z + k, NZ)].astype(F32)
    crcv[c] = total
    v_c = send(VC, "c", lambda there: crcv.at[c], crcv.at[c], crcv.at[0])
    q_y.wait_recv()
    total = qry[0]
    for k in range(1, NY):
        total = total + qry[k]
    qrz[z] = total
    q_z = send(QZ, "z", lambda there: qrz.at[z], qrz.at[z], qrz.at[0 : NZ - 1])
    v_c.wait_recv()
    xrcv[x] = crcv[0] + crcv[1]
    v_x = send(VX, "x", lambda there: xrcv.at[x], xrcv.at[x], xrcv.at[0 : NX - 1])
    v_x.wait_recv()
    vall[y] = ((xrcv[0] + xrcv[1]) + (xrcv[2] + xrcv[3])).astype(BF16)
    v_y = send(VY, "y", lambda there: vall.at[y], vall.at[y], vall.at[0 : NY - 1])
    q_z.wait_recv()
    total = qrz[0]
    for k in range(1, NZ):
        total = total + qrz[k]
    last[...] = total
    mine = last[pl.ds(y * OWN, OWN), :]
    for t in range(TILTS):
        wg_out[t] = pltpu.roll(mine, (COLS - CTRL * t) % COLS, 1)[:, 0:CTRL]
    v_y.wait_recv()
    back_out[...] = jnp.transpose(vall[...].astype(F32).reshape(COLS, SLAB))
    pltpu.make_async_copy(rb, res_out, lsem.at[7]).wait()
    for copy in sent:
        copy.wait_send()


def hand_over(res_in, grad_in, back_in, res_out, grad_out, back_out, res, grad, back, isem, osem):
    part = PARTS // 8
    ways = [(grad_in, grad, grad_out), (back_in, back, back_out)]
    for k in range(8):
        rows = pl.ds(k * part, part)
        ways.append((res_in.at[rows], res.at[rows], res_out.at[rows]))
    inward = [pltpu.make_async_copy(a, b, isem.at[k]) for k, (a, b, _) in enumerate(ways)]
    outward = [pltpu.make_async_copy(b, c, osem.at[k]) for k, (_, b, c) in enumerate(ways)]
    for copy in inward:
        copy.start()
    for first, second in zip(inward, outward):
        first.wait()
        second.start()
    for copy in outward:
        copy.wait()


def shards(reference_volume, cell_index, cell_frac, warp, series, position, images):
    vmem = pl.BlockSpec(memory_space=pltpu.VMEM)
    hbm = pl.BlockSpec(memory_space=pl.ANY)
    scratch = [
        pltpu.VMEM((SLAB, COLS), BF16),
        pltpu.VMEM((TILTS, OWN, BOX), jnp.int32),
        pltpu.VMEM((TILTS, OWN, BOX), F32),
        pltpu.VMEM((TILTS, OWN, CTRL), BF16),
        pltpu.VMEM((PARTS,), jnp.int32),
        pltpu.VMEM((PARTS,), F32),
        pltpu.VMEM((PARTS, TILTS, BAND, COLS), BF16),
        pltpu.VMEM((PARTS * ROWS, COLS), F32),
        pltpu.VMEM((ROWS, PARTS, COLS), BF16),
        pltpu.VMEM((3, 8, COLS), F32),
        pltpu.VMEM((NC, NX, NY, 8, COLS), F32),
        pltpu.VMEM((OWN * TILTS, NZ, BAND, COLS), F32),
        pltpu.VMEM((NZ, OWN * TILTS, BAND, COLS), F32),
        pltpu.VMEM((NC, NX, NY, OWN * ROWS, COLS), BF16),
        pltpu.VMEM((GROUP * ROWS, COLS), F32),
        pltpu.VMEM((NS * ROWS, COLS), F32),
        pltpu.VMEM((NC * NX, ROWS + 1, GROUP, COLS), F32),
        pltpu.VMEM((NX, ROWS + 1, GROUP, COLS), F32),
        pltpu.VMEM((NX, ROWS + 1, GROUP, COLS), F32),
        pltpu.VMEM((NY, CPY, ROWS * GROUP), BF16),
        pltpu.VMEM((NY, CPY, ROWS * GROUP), BF16),
        pltpu.VMEM((ROWS * GROUP, CELLS), BF16),
        pltpu.VMEM((NZ, CPY, SLAB), BF16),
        pltpu.VMEM((NZ, CPY, SLAB), BF16),
        pltpu.VMEM((NC, CPY, SLAB), F32),
        pltpu.VMEM((NX, CPY, SLAB), F32),
        pltpu.VMEM((NY, CPY, SLAB), BF16),
        pltpu.VMEM((NC, NX, GROUP, COLS), F32),
        pltpu.VMEM((NX, GROUP, COLS), F32),
        pltpu.VMEM((NX, GROUP, COLS), F32),
        pltpu.VMEM((NY, GROUP, COLS), F32),
        pltpu.VMEM((NZ, GROUP, COLS), F32),
        pltpu.VMEM((GROUP, COLS), F32),
        pltpu.VMEM((PARTS * ROWS, COLS), F32),
        pltpu.VMEM((PARTS, TILTS, BAND, COLS), BF16),
        pltpu.SemaphoreType.DMA((LAST + NX,)),
        pltpu.SemaphoreType.DMA((LAST + NX,)),
        pltpu.SemaphoreType.DMA((8,)),
    ]
    residual, warp_grad, back_volume = pl.pallas_call(
        kernel,
        out_shape=(
            jax.ShapeDtypeStruct((PARTS, TILTS, BAND, COLS), BF16),
            jax.ShapeDtypeStruct((TILTS, OWN, CTRL), F32),
            jax.ShapeDtypeStruct((SLAB, COLS), F32),
        ),
        in_specs=[hbm] * 7,
        out_specs=(hbm, vmem, vmem),
        scratch_shapes=scratch,
        compiler_params=pltpu.CompilerParams(
            collective_id=0, has_side_effects=True, vmem_limit_bytes=56 << 20
        ),
        name="refine",
    )(
        reference_volume,
        jnp.transpose(cell_index, (1, 0, 2)),
        jnp.transpose(cell_frac, (1, 0, 2)),
        jnp.transpose(warp, (2, 1, 0)),
        series,
        position,
        images,
    )
    residual, warp_grad, back_volume = pl.pallas_call(
        hand_over,
        out_shape=(
            jax.ShapeDtypeStruct(residual.shape, BF16),
            jax.ShapeDtypeStruct(warp_grad.shape, F32),
            jax.ShapeDtypeStruct(back_volume.shape, F32),
        ),
        in_specs=[hbm] * 3,
        out_specs=(hbm, hbm, hbm),
        scratch_shapes=[
            pltpu.VMEM(residual.shape, BF16),
            pltpu.VMEM(warp_grad.shape, F32),
            pltpu.VMEM(back_volume.shape, F32),
            pltpu.SemaphoreType.DMA((10,)),
            pltpu.SemaphoreType.DMA((10,)),
        ],
        name="hand_over",
    )(residual, warp_grad, back_volume)
    return residual, jnp.transpose(warp_grad, (2, 1, 0)), back_volume


def solution(mesh):
    placed = (
        P("slab", None),
        P("dom", None, None),
        P("dom", None, None),
        P(None, "dom", None),
        P("dom"),
        P("dom"),
        P("dom", None, "slab", None),
    )
    return jax.shard_map(
        shards,
        mesh=mesh,
        in_specs=placed,
        out_specs=(P("dom", None, "slab", None), P(None, "dom", None), P("slab", None)),
        check_vma=False,
    )
```

```python
import jax
import jax.numpy as jnp
from jax import lax
from jax.experimental import pallas as pl
from jax.experimental.pallas import tpu as pltpu
from jax.sharding import PartitionSpec as P

MESH = pl.DeviceIdType.MESH
F32, BF16 = jnp.float32, jnp.bfloat16
NY, NX, NC, NZ = 8, 4, 2, 8
BOX, TILTS, CTRL, COLS = 64, 3, 4, 128
PARTS = 256
BAND = BOX // NZ
ROWS = TILTS * BAND
OWN = 2
NS = NY * NX * NC * OWN
GROUP = NY * OWN
SLAB = BOX * BOX // NZ
CELLS = BOX * BOX
CPY = COLS // NY

(META_Y, META_X, META_C, PZ, PY, PX, PC, VZ, VC, VX, VY, QC, QX, QY, QZ) = range(15)
SC, SX, SY, EXCHANGES = 15, 15 + TILTS, 15 + 2 * TILTS, 15 + 3 * TILTS


def split2(v):
    hi = v.astype(BF16)
    return hi, (v - hi.astype(F32)).astype(BF16)


def split3(v):
    hi = v.astype(BF16)
    rest = v - hi.astype(F32)
    mid = rest.astype(BF16)
    return hi, mid, (rest - mid.astype(F32)).astype(BF16)


def dot(a, b):
    return jnp.dot(a, b, preferred_element_type=F32)


def kernel(
    vol_in,
    idx_in,
    frac_in,
    warp_in,
    series_in,
    pos_in,
    images,
    res_out,
    wg_out,
    back_out,
    vol,
    idx,
    frac,
    warp,
    series,
    pos,
    imgv,
    xf,
    xt,
    tmp,
    meta,
    psrc,
    prcv,
    pall,
    pgf,
    pf,
    bs,
    brc,
    brx,
    ysrc,
    yrcv,
    wsp,
    zsrc,
    zrcv,
    crcv,
    xrcv,
    vall,
    qsrc,
    qrc,
    qrx,
    qry,
    qrz,
    last,
    rf,
    rb,
    ssem,
    rsem,
    lsem,
):
    d, z = lax.axis_index("dom"), lax.axis_index("slab")
    c, x, y = lax.rem(d, NC), lax.rem(d // NC, NX), d // (NC * NX)

    def spot(axis, k):
        at = {"y": y, "x": x, "c": c, "z": z}
        size = {"y": NY, "x": NX, "c": NC, "z": NZ}[axis]
        at[axis] = lax.rem(at[axis] + k, size)
        return ((at["y"] * NX + at["x"]) * NC + at["c"], at["z"]), at[axis]

    def remote(row, device, src, dst):
        return pltpu.make_async_remote_copy(
            src_ref=src,
            dst_ref=dst,
            send_sem=ssem.at[row],
            recv_sem=rsem.at[row],
            device_id=device,
            device_id_type=MESH,
        )

    def send(row, axis, src, dst, bulk):
        size = {"y": NY, "x": NX, "c": NC, "z": NZ}[axis]
        for k in range(1, size):
            device, there = spot(axis, k)
            remote(row, device, src(there), dst).start()
        whole = remote(row, spot(axis, 1)[0], bulk, bulk)
        sent.append(whole)
        return whole

    sent = []

    barrier = pltpu.get_barrier_semaphore()
    partners = [spot(axis, k)[0] for axis, size in (("c", NC), ("z", NZ)) for k in range(1, size)]
    plane = []
    for j in range(1, NY * NX):
        there = lax.rem(y + j // NX, NY) * NX + lax.rem(x + j % NX, NX)
        plane.append((there * NC + c, z))
    for device in partners + plane:
        pl.semaphore_signal(barrier, inc=1, device_id=device, device_id_type=MESH)

    small_copies = [
        pltpu.make_async_copy(a, b, lsem.at[k])
        for k, (a, b) in enumerate(
            (
                (idx_in, idx),
                (frac_in, frac),
                (warp_in, warp),
                (vol_in, vol),
                (series_in, series),
                (pos_in, pos),
            )
        )
    ]
    for copy in small_copies:
        copy.start()
    step = PARTS // 8
    for k in range(8):
        rows = pl.ds(k * step, step)
        pltpu.make_async_copy(images.at[rows], imgv.at[rows], lsem.at[6]).start()

    lane8 = lax.broadcasted_iota(jnp.int32, (8, COLS), 1)
    tmp[...] = jnp.zeros_like(tmp)
    for copy in small_copies[:3]:
        copy.wait()
    for q in range(OWN):
        for t in range(TILTS):
            at = q * 4 + t
            tmp[0, at : at + 1, 0:BOX] = idx[t, q : q + 1].astype(F32)
            tmp[1, at : at + 1, 0:BOX] = frac[t, q : q + 1]
            tmp[2, at : at + 1, 0:CTRL] = warp[t].astype(F32)[q : q + 1]
    own_idx, own_frac, own_warp = tmp[0], tmp[1], tmp[2]
    band_idx = pltpu.roll(own_idx, lax.rem(COLS - z * BAND, COLS), 1)
    band_frac = pltpu.roll(own_frac, lax.rem(COLS - z * BAND + BAND, COLS), 1)
    rolled_warp = pltpu.roll(own_warp, 2 * BAND, 1)
    own_at = x * NY + y
    meta[c, own_at] = jnp.where(
        lane8 < BAND, band_idx, jnp.where(lane8 < 2 * BAND, band_frac, rolled_warp)
    )

    pl.semaphore_wait(barrier, len(partners + plane))
    for device in plane:
        remote(META_Y, device, meta.at[c, own_at], meta.at[c, own_at]).start()
    meta_p = remote(META_Y, plane[0], meta.at[0, 1:], meta.at[0, 1:])
    sent.append(meta_p)

    columns = jnp.transpose(jnp.where(lane8 < BOX, own_idx, pltpu.roll(own_frac, BOX, 1)))
    cell = (lax.broadcasted_iota(jnp.int32, (BOX, SLAB), 1) + z * SLAB).astype(F32)
    small_copies[3].wait()
    volume = vol[...]
    for q in range(OWN):
        for t in range(TILTS):
            low = columns[0:BOX, q * 4 + t : q * 4 + t + 1]
            part = columns[BOX : 2 * BOX, q * 4 + t : q * 4 + t + 1]
            weight = jnp.where(cell == low, 1.0 - part, 0.0) + jnp.where(cell == low + BOX, part, 0.0)
            hi, mid, lo = split3(weight)
            value = dot(hi, volume) + (dot(mid, volume) + dot(lo, volume))
            psrc[q * TILTS + t] = value.reshape(NZ, BAND, COLS)

    p_z = send(PZ, "z", lambda there: psrc.at[:, there], prcv.at[z], prcv.at[0 : NZ - 1])

    pltpu.make_async_copy(images, imgv, lsem.at[6]).wait()
    for copy in small_copies[4:]:
        copy.wait()

    def widen(i, _):
        part = imgv[pl.ds(i * 32, 32)].astype(F32)
        xf[pl.ds(pl.multiple_of(i * 32 * ROWS, 32 * ROWS), 32 * ROWS), :] = part.reshape(32 * ROWS, COLS)
        return 0

    lax.fori_loop(0, PARTS // 32, widen, 0)

    def gather_rows(r, _):
        xt[r] = xf[pl.ds(r, PARTS, stride=ROWS), :].astype(BF16)
        return 0

    lax.fori_loop(0, ROWS, gather_rows, 0)

    row = lax.broadcasted_iota(jnp.int32, (NS, PARTS), 0)
    name = (
        lax.rem(row, GROUP) // OWN * (NX * NC * OWN)
        + lax.rem(row // GROUP, NX) * (NC * OWN)
        + row // (GROUP * NX) * OWN
        + lax.rem(row, OWN)
    )
    hit = series[...].reshape(1, PARTS) == name
    hot = hit.astype(F32)
    hot16 = hot.astype(BF16)
    at = pos[...].reshape(1, PARTS)
    remain = 1.0 - at
    square = at * at
    cubed = square * at
    basis = [
        remain * remain * remain / 6.0,
        (3.0 * cubed - 6.0 * square + 4.0) / 6.0,
        (-3.0 * cubed + 3.0 * square + 3.0 * at + 1.0) / 6.0,
        cubed / 6.0,
    ]

    meta_p.wait_recv()
    meta_c = send(META_C, "c", lambda there: meta.at[c], meta.at[c], meta.at[0])
    meta_c.wait_recv()

    flat_meta = meta.reshape(NS * 4, COLS)
    lane = lax.broadcasted_iota(jnp.int32, (NS, COLS), 1)
    table = jnp.zeros((NS, COLS), F32)
    for t in range(TILTS):
        rows = pltpu.roll(flat_meta[pl.ds(t, NS, stride=4), :], COLS - 2 * BAND + CTRL * t, 1)
        table = jnp.where(lane // CTRL == t, rows, table)
    chosen = dot(jnp.transpose(table)[0:16].astype(BF16), hot16)
    scale = [
        sum(basis[k] * chosen[CTRL * t + k : CTRL * t + k + 1] for k in range(CTRL))
        for t in range(TILTS)
    ]

    other, there = spot("c", 1)
    c_copies, s_x, s_y = [], [], []
    for t in range(TILTS):
        weight = jnp.where(hit, scale[t], 0.0)
        squares = jnp.sum(weight * weight, axis=1, keepdims=True)
        both = jnp.concatenate(split2(weight), axis=0)
        for u in range(0, BAND, 2):
            r = t * BAND + u
            pair = dot(both, jnp.concatenate([xt[r], xt[r + 1]], axis=1))
            pair = pair[:NS] + pair[NS:]
            bs[:, t, u] = pair[:, :COLS].reshape(NC * NX, GROUP, COLS)
            bs[:, t, u + 1] = pair[:, COLS:].reshape(NC * NX, GROUP, COLS)
        bs[:, t, BAND] = jnp.broadcast_to(squares, (NS, COLS)).reshape(NC * NX, GROUP, COLS)
        c_copies.append(remote(SC + t, other, bs.at[pl.ds(there * NX, NX), t], brc.at[:, t]))
        c_copies[t].start()

    p_z.wait_recv()
    own = psrc[:, z]
    for k in range(1, NZ):
        own = own + prcv[lax.rem(z + k, NZ)]
    pall[c, x, y] = own.reshape(OWN * ROWS, COLS).astype(BF16)
    p_y = send(PY, "y", lambda there: pall.at[c, x, y], pall.at[c, x, y], pall.at[0, 0, 0 : NY - 1])


    for t in range(TILTS):
        c_copies[t].wait_recv()
        brc[:, t] = brc[:, t] + bs[pl.ds(c * NX, NX), t]
        bulk = brx.at[0 : NX - 1, t]
        s_x.append(
            send(SX + t, "x", lambda there: brc.at[there, t], brx.at[x, t], bulk)
        )
    sent += c_copies

    p_y.wait_recv()
    p_x = send(PX, "x", lambda there: pall.at[c, x], pall.at[c, x], pall.at[0, 0 : NX - 1])
    pgf[...] = pall[c, x].reshape(GROUP * ROWS, COLS).astype(F32)

    flat_group = meta.at[c, pl.ds(x * NY, NY)].reshape(NY * 8, COLS)
    cells = lax.broadcasted_iota(jnp.int32, (GROUP, CELLS), 1).astype(F32)
    for t in range(TILTS):
        group = flat_group[pl.ds(t, GROUP, stride=4), :]
        for u in range(BAND):
            low = group[:, u : u + 1]
            part = group[:, BAND + u : BAND + u + 1]
            weight = jnp.where(
                cells == low, 1.0 - part, jnp.where(cells == low + BOX, part, 0.0)
            )
            wsp[(t * BAND + u) * GROUP : (t * BAND + u + 1) * GROUP, :] = weight.astype(BF16)

    for t in range(TILTS):
        s_x[t].wait_recv()
        total = brc[x, t]
        for k in range(1, NX):
            total = total + brx[lax.rem(x + k, NX), t]
        fixed = []
        for u in range(BAND):
            guess = pgf[pl.ds(t * BAND + u, GROUP, stride=ROWS), :]
            fixed.append(total[u] - total[BAND] * guess)
        turned = jnp.transpose(jnp.concatenate(fixed, axis=0))
        ysrc[t] = turned.reshape(NY, CPY, BAND * GROUP).astype(BF16)
        bulk = yrcv.at[t, 0 : NY - 1]
        s_y.append(
            send(SY + t, "y", lambda there: ysrc.at[t, there], yrcv.at[t, y], bulk)
        )

    hot_turned = jnp.transpose(hot).astype(BF16)
    lane_p = lax.broadcasted_iota(jnp.int32, (PARTS, COLS), 1)
    factors = jnp.transpose(jnp.concatenate(scale + basis + [basis[0]], axis=0))
    inner = jnp.zeros((PARTS, COLS), F32)

    p_x.wait_recv()
    p_c = send(PC, "c", lambda there: pall.at[c], pall.at[c], pall.at[0])
    totals = []
    for t in range(TILTS):
        s_y[t].wait_recv()
        total = ysrc[t, y].astype(F32)
        for k in range(1, NY):
            total = total + yrcv[t, lax.rem(y + k, NY)].astype(F32)
        totals.append(total)
    total = jnp.concatenate(totals, axis=1)
    both = jnp.concatenate(split2(total), axis=0)
    for k in range(NZ):
        part = dot(both, wsp[:, k * SLAB : (k + 1) * SLAB])
        zsrc[k] = (part[:CPY] + part[CPY:]).astype(BF16)
    v_z = send(VZ, "z", lambda there: zsrc.at[there], zrcv.at[z], zrcv.at[0 : NZ - 1])

    p_c.wait_recv()
    pf[...] = pall[...].reshape(NS * ROWS, COLS).astype(F32)
    for t in range(TILTS):
        scale_column = factors[:, t : t + 1]
        acc = jnp.zeros((PARTS, COLS), F32)
        for u in range(0, BAND, 2):
            r = t * BAND + u
            pair = [pf[pl.ds(r + k, NS, stride=ROWS), :].astype(BF16) for k in range(2)]
            guesses = dot(hot_turned, jnp.concatenate(pair, axis=1))
            for k in range(2):
                guess = guesses[:, k * COLS : (k + 1) * COLS]
                left = (xt[r + k].astype(F32) - scale_column * guess).astype(BF16).astype(F32)
                rf[(r + k) * PARTS : (r + k + 1) * PARTS, :] = left
                acc = acc + left * guess
        inner = jnp.where(lane_p // CTRL == t, jnp.sum(acc, axis=1, keepdims=True), inner)

    def narrow(i, _):
        for k in range(16):
            part = rf[pl.ds(i * 16 + k, ROWS, stride=PARTS), :]
            rb[i * 16 + k] = part.reshape(TILTS, BAND, COLS).astype(BF16)
        return 0

    lax.fori_loop(0, PARTS // 16, narrow, 0)
    for k in range(8):
        rows = pl.ds(k * step, step)
        pltpu.make_async_copy(rb.at[rows], res_out.at[rows], lsem.at[7]).start()
    term = jnp.zeros((PARTS, COLS), F32)
    for k in range(CTRL):
        term = jnp.where(lax.rem(lane_p, CTRL) == k, factors[:, TILTS + k : TILTS + k + 1] * inner, term)
    hi, mid, lo = split3(term)
    grad = (dot(hot16, hi) + (dot(hot16, mid) + dot(hot16, lo))) * (-1.0 / (BOX * BOX))
    qsrc[...] = grad.reshape(NC, NX, GROUP, COLS)
    q_c = send(QC, "c", lambda there: qsrc.at[there], qrc, qrc)

    q_c.wait_recv()
    qrc[...] = qrc[...] + qsrc[c]
    q_x = send(QX, "x", lambda there: qrc.at[there], qrx.at[x], qrx.at[0 : NX - 1])
    v_z.wait_recv()
    total = zsrc[z].astype(F32)
    for k in range(1, NZ):
        total = total + zrcv[lax.rem(z + k, NZ)].astype(F32)
    crcv[c] = total
    v_c = send(VC, "c", lambda there: crcv.at[c], crcv.at[c], crcv.at[0])
    v_c.wait_recv()
    xrcv[x] = crcv[0] + crcv[1]
    v_x = send(VX, "x", lambda there: xrcv.at[x], xrcv.at[x], xrcv.at[0 : NX - 1])
    q_x.wait_recv()
    total = qrc[x]
    for k in range(1, NX):
        total = total + qrx[lax.rem(x + k, NX)]
    qry[y] = total
    q_y = send(QY, "y", lambda there: qry.at[y], qry.at[y], qry.at[0 : NY - 1])
    v_x.wait_recv()
    vall[y] = ((xrcv[0] + xrcv[1]) + (xrcv[2] + xrcv[3])).astype(BF16)
    v_y = send(VY, "y", lambda there: vall.at[y], vall.at[y], vall.at[0 : NY - 1])
    q_y.wait_recv()
    total = qry[0]
    for k in range(1, NY):
        total = total + qry[k]
    qrz[z] = total
    q_z = send(QZ, "z", lambda there: qrz.at[z], qrz.at[z], qrz.at[0 : NZ - 1])
    q_z.wait_recv()
    total = qrz[0]
    for k in range(1, NZ):
        total = total + qrz[k]
    last[...] = total
    mine = last[pl.ds(y * OWN, OWN), :]
    for t in range(TILTS):
        wg_out[t] = pltpu.roll(mine, (COLS - CTRL * t) % COLS, 1)[:, 0:CTRL]
    v_y.wait_recv()
    back_out[...] = jnp.transpose(vall[...].astype(F32).reshape(COLS, SLAB))
    pltpu.make_async_copy(rb, res_out, lsem.at[7]).wait()
    for copy in sent:
        copy.wait_send()


def hand_over(res_in, grad_in, back_in, res_out, grad_out, back_out, res, grad, back, isem, osem):
    part = PARTS // 8
    ways = [(grad_in, grad, grad_out), (back_in, back, back_out)]
    for k in range(8):
        rows = pl.ds(k * part, part)
        ways.append((res_in.at[rows], res.at[rows], res_out.at[rows]))
    inward = [pltpu.make_async_copy(a, b, isem.at[k]) for k, (a, b, _) in enumerate(ways)]
    outward = [pltpu.make_async_copy(b, c, osem.at[k]) for k, (_, b, c) in enumerate(ways)]
    for copy in inward:
        copy.start()
    for first, second in zip(inward, outward):
        first.wait()
        second.start()
    for copy in outward:
        copy.wait()


def shards(reference_volume, cell_index, cell_frac, warp, series, position, images):
    vmem = pl.BlockSpec(memory_space=pltpu.VMEM)
    hbm = pl.BlockSpec(memory_space=pl.ANY)
    scratch = [
        pltpu.VMEM((SLAB, COLS), BF16),
        pltpu.VMEM((TILTS, OWN, BOX), jnp.int32),
        pltpu.VMEM((TILTS, OWN, BOX), F32),
        pltpu.VMEM((TILTS, OWN, CTRL), BF16),
        pltpu.VMEM((PARTS,), jnp.int32),
        pltpu.VMEM((PARTS,), F32),
        pltpu.VMEM((PARTS, TILTS, BAND, COLS), BF16),
        pltpu.VMEM((PARTS * ROWS, COLS), F32),
        pltpu.VMEM((ROWS, PARTS, COLS), BF16),
        pltpu.VMEM((3, 8, COLS), F32),
        pltpu.VMEM((NC, NX * NY, 8, COLS), F32),
        pltpu.VMEM((OWN * TILTS, NZ, BAND, COLS), F32),
        pltpu.VMEM((NZ, OWN * TILTS, BAND, COLS), F32),
        pltpu.VMEM((NC, NX, NY, OWN * ROWS, COLS), BF16),
        pltpu.VMEM((GROUP * ROWS, COLS), F32),
        pltpu.VMEM((NS * ROWS, COLS), F32),
        pltpu.VMEM((NC * NX, TILTS, BAND + 1, GROUP, COLS), F32),
        pltpu.VMEM((NX, TILTS, BAND + 1, GROUP, COLS), F32),
        pltpu.VMEM((NX, TILTS, BAND + 1, GROUP, COLS), F32),
        pltpu.VMEM((TILTS, NY, CPY, BAND * GROUP), BF16),
        pltpu.VMEM((TILTS, NY, CPY, BAND * GROUP), BF16),
        pltpu.VMEM((ROWS * GROUP, CELLS), BF16),
        pltpu.VMEM((NZ, CPY, SLAB), BF16),
        pltpu.VMEM((NZ, CPY, SLAB), BF16),
        pltpu.VMEM((NC, CPY, SLAB), F32),
        pltpu.VMEM((NX, CPY, SLAB), F32),
        pltpu.VMEM((NY, CPY, SLAB), BF16),
        pltpu.VMEM((NC, NX, GROUP, COLS), F32),
        pltpu.VMEM((NX, GROUP, COLS), F32),
        pltpu.VMEM((NX, GROUP, COLS), F32),
        pltpu.VMEM((NY, GROUP, COLS), F32),
        pltpu.VMEM((NZ, GROUP, COLS), F32),
        pltpu.VMEM((GROUP, COLS), F32),
        pltpu.VMEM((PARTS * ROWS, COLS), F32),
        pltpu.VMEM((PARTS, TILTS, BAND, COLS), BF16),
        pltpu.SemaphoreType.DMA((EXCHANGES,)),
        pltpu.SemaphoreType.DMA((EXCHANGES,)),
        pltpu.SemaphoreType.DMA((8,)),
    ]
    residual, warp_grad, back_volume = pl.pallas_call(
        kernel,
        out_shape=(
            jax.ShapeDtypeStruct((PARTS, TILTS, BAND, COLS), BF16),
            jax.ShapeDtypeStruct((TILTS, OWN, CTRL), F32),
            jax.ShapeDtypeStruct((SLAB, COLS), F32),
        ),
        in_specs=[hbm] * 7,
        out_specs=(hbm, vmem, vmem),
        scratch_shapes=scratch,
        compiler_params=pltpu.CompilerParams(
            collective_id=0, has_side_effects=True, vmem_limit_bytes=56 << 20
        ),
        name="refine",
    )(
        reference_volume,
        jnp.transpose(cell_index, (1, 0, 2)),
        jnp.transpose(cell_frac, (1, 0, 2)),
        jnp.transpose(warp, (2, 1, 0)),
        series,
        position,
        images,
    )
    residual, warp_grad, back_volume = pl.pallas_call(
        hand_over,
        out_shape=(
            jax.ShapeDtypeStruct(residual.shape, BF16),
            jax.ShapeDtypeStruct(warp_grad.shape, F32),
            jax.ShapeDtypeStruct(back_volume.shape, F32),
        ),
        in_specs=[hbm] * 3,
        out_specs=(hbm, hbm, hbm),
        scratch_shapes=[
            pltpu.VMEM(residual.shape, BF16),
            pltpu.VMEM(warp_grad.shape, F32),
            pltpu.VMEM(back_volume.shape, F32),
            pltpu.SemaphoreType.DMA((10,)),
            pltpu.SemaphoreType.DMA((10,)),
        ],
        name="hand_over",
    )(residual, warp_grad, back_volume)
    return residual, jnp.transpose(warp_grad, (2, 1, 0)), back_volume


def solution(mesh):
    placed = (
        P("slab", None),
        P("dom", None, None),
        P("dom", None, None),
        P(None, "dom", None),
        P("dom"),
        P("dom"),
        P("dom", None, "slab", None),
    )
    return jax.shard_map(
        shards,
        mesh=mesh,
        in_specs=placed,
        out_specs=(P("dom", None, "slab", None), P(None, "dom", None), P("slab", None)),
        check_vma=False,
    )
```

```python
import jax
import jax.numpy as jnp
from jax import lax
from jax.experimental import pallas as pl
from jax.experimental.pallas import tpu as pltpu
from jax.sharding import PartitionSpec as P

MESH = pl.DeviceIdType.MESH
F32, BF16 = jnp.float32, jnp.bfloat16
NY, NX, NC, NZ = 8, 4, 2, 8
BOX, TILTS, CTRL, COLS = 64, 3, 4, 128
PARTS = 256
BAND = BOX // NZ
ROWS = TILTS * BAND
OWN = 2
NS = NY * NX * NC * OWN
GROUP = NY * OWN
SLAB = BOX * BOX // NZ
CELLS = BOX * BOX
CPY = COLS // NY

(META_Y, META_X, META_C, PZ, PY, PX, PC, VZ, VC, VX, VY, QC, QX, QY, QZ, PXY) = range(16)
SC, SX, SY, EXCHANGES = 16, 16 + TILTS, 16 + 2 * TILTS, 16 + 3 * TILTS


def split2(v):
    hi = v.astype(BF16)
    return hi, (v - hi.astype(F32)).astype(BF16)


def split3(v):
    hi = v.astype(BF16)
    rest = v - hi.astype(F32)
    mid = rest.astype(BF16)
    return hi, mid, (rest - mid.astype(F32)).astype(BF16)


def dot(a, b):
    return jnp.dot(a, b, preferred_element_type=F32)


def kernel(
    vol_in,
    idx_in,
    frac_in,
    warp_in,
    series_in,
    pos_in,
    images,
    res_out,
    wg_out,
    back_out,
    vol,
    idx,
    frac,
    warp,
    series,
    pos,
    imgv,
    xf,
    xt,
    tmp,
    meta,
    psrc,
    prcv,
    pall,
    pgf,
    pf,
    bs,
    brc,
    brx,
    ysrc,
    yrcv,
    wsp,
    zsrc,
    zrcv,
    crcv,
    xrcv,
    vall,
    qsrc,
    qrc,
    qrx,
    qry,
    qrz,
    last,
    rf,
    rb,
    ssem,
    rsem,
    lsem,
):
    d, z = lax.axis_index("dom"), lax.axis_index("slab")
    c, x, y = lax.rem(d, NC), lax.rem(d // NC, NX), d // (NC * NX)

    def spot(axis, k):
        at = {"y": y, "x": x, "c": c, "z": z}
        size = {"y": NY, "x": NX, "c": NC, "z": NZ}[axis]
        at[axis] = lax.rem(at[axis] + k, size)
        return ((at["y"] * NX + at["x"]) * NC + at["c"], at["z"]), at[axis]

    def remote(row, device, src, dst):
        return pltpu.make_async_remote_copy(
            src_ref=src,
            dst_ref=dst,
            send_sem=ssem.at[row],
            recv_sem=rsem.at[row],
            device_id=device,
            device_id_type=MESH,
        )

    def send(row, axis, src, dst, bulk):
        size = {"y": NY, "x": NX, "c": NC, "z": NZ}[axis]
        for k in sorted(range(1, size), key=lambda k: -min(k, size - k)):
            device, there = spot(axis, k)
            remote(row, device, src(there), dst).start()
        whole = remote(row, spot(axis, 1)[0], bulk, bulk)
        sent.append(whole)
        return whole

    sent = []

    barrier = pltpu.get_barrier_semaphore()
    partners = [spot(axis, k)[0] for axis, size in (("c", NC), ("z", NZ)) for k in range(1, size)]
    plane = []
    steps = [min(j // NX, NY - j // NX) + min(j % NX, NX - j % NX) for j in range(NY * NX)]
    for j in sorted(range(1, NY * NX), key=lambda j: -steps[j]):
        there = lax.rem(y + j // NX, NY) * NX + lax.rem(x + j % NX, NX)
        plane.append((there * NC + c, z))
    for device in partners + plane:
        pl.semaphore_signal(barrier, inc=1, device_id=device, device_id_type=MESH)

    small_copies = [
        pltpu.make_async_copy(a, b, lsem.at[k])
        for k, (a, b) in enumerate(
            (
                (idx_in, idx),
                (frac_in, frac),
                (warp_in, warp),
                (vol_in, vol),
                (series_in, series),
                (pos_in, pos),
            )
        )
    ]
    for copy in small_copies:
        copy.start()
    step = PARTS // 8
    for k in range(8):
        rows = pl.ds(k * step, step)
        pltpu.make_async_copy(images.at[rows], imgv.at[rows], lsem.at[6]).start()

    lane8 = lax.broadcasted_iota(jnp.int32, (8, COLS), 1)
    tmp[...] = jnp.zeros_like(tmp)
    for copy in small_copies[:3]:
        copy.wait()
    for q in range(OWN):
        for t in range(TILTS):
            at = q * 4 + t
            tmp[0, at : at + 1, 0:BOX] = idx[t, q : q + 1].astype(F32)
            tmp[1, at : at + 1, 0:BOX] = frac[t, q : q + 1]
            tmp[2, at : at + 1, 0:CTRL] = warp[t].astype(F32)[q : q + 1]
    own_idx, own_frac, own_warp = tmp[0], tmp[1], tmp[2]
    band_idx = pltpu.roll(own_idx, lax.rem(COLS - z * BAND, COLS), 1)
    band_frac = pltpu.roll(own_frac, lax.rem(COLS - z * BAND + BAND, COLS), 1)
    rolled_warp = pltpu.roll(own_warp, 2 * BAND, 1)
    own_at = x * NY + y
    meta[c, own_at] = jnp.where(
        lane8 < BAND, band_idx, jnp.where(lane8 < 2 * BAND, band_frac, rolled_warp)
    )

    pl.semaphore_wait(barrier, len(partners + plane))
    for device in plane:
        remote(META_Y, device, meta.at[c, own_at], meta.at[c, own_at]).start()
    meta_p = remote(META_Y, plane[0], meta.at[0, 1:], meta.at[0, 1:])
    sent.append(meta_p)

    columns = jnp.transpose(jnp.where(lane8 < BOX, own_idx, pltpu.roll(own_frac, BOX, 1)))
    cell = (lax.broadcasted_iota(jnp.int32, (BOX, SLAB), 1) + z * SLAB).astype(F32)
    small_copies[3].wait()
    volume = vol[...]
    for q in range(OWN):
        for t in range(TILTS):
            low = columns[0:BOX, q * 4 + t : q * 4 + t + 1]
            part = columns[BOX : 2 * BOX, q * 4 + t : q * 4 + t + 1]
            weight = jnp.where(cell == low, 1.0 - part, 0.0) + jnp.where(cell == low + BOX, part, 0.0)
            hi, mid, lo = split3(weight)
            value = dot(hi, volume) + (dot(mid, volume) + dot(lo, volume))
            psrc[q * TILTS + t] = value.reshape(NZ, BAND, COLS)

    p_z = send(PZ, "z", lambda there: psrc.at[:, there], prcv.at[z], prcv.at[0 : NZ - 1])

    pltpu.make_async_copy(images, imgv, lsem.at[6]).wait()
    for copy in small_copies[4:]:
        copy.wait()

    def widen(i, _):
        part = imgv[pl.ds(i * 32, 32)].astype(F32)
        xf[pl.ds(pl.multiple_of(i * 32 * ROWS, 32 * ROWS), 32 * ROWS), :] = part.reshape(32 * ROWS, COLS)
        return 0

    lax.fori_loop(0, PARTS // 32, widen, 0)

    def gather_rows(r, _):
        xt[r] = xf[pl.ds(r, PARTS, stride=ROWS), :].astype(BF16)
        return 0

    lax.fori_loop(0, ROWS, gather_rows, 0)

    row = lax.broadcasted_iota(jnp.int32, (NS, PARTS), 0)
    name = (
        lax.rem(row, GROUP) // OWN * (NX * NC * OWN)
        + lax.rem(row // GROUP, NX) * (NC * OWN)
        + row // (GROUP * NX) * OWN
        + lax.rem(row, OWN)
    )
    hit = series[...].reshape(1, PARTS) == name
    hot = hit.astype(F32)
    hot16 = hot.astype(BF16)
    at = pos[...].reshape(1, PARTS)
    remain = 1.0 - at
    square = at * at
    cubed = square * at
    basis = [
        remain * remain * remain / 6.0,
        (3.0 * cubed - 6.0 * square + 4.0) / 6.0,
        (-3.0 * cubed + 3.0 * square + 3.0 * at + 1.0) / 6.0,
        cubed / 6.0,
    ]

    meta_p.wait_recv()
    meta_c = send(META_C, "c", lambda there: meta.at[c], meta.at[c], meta.at[0])
    meta_c.wait_recv()

    flat_meta = meta.reshape(NS * 4, COLS)
    lane = lax.broadcasted_iota(jnp.int32, (NS, COLS), 1)
    table = jnp.zeros((NS, COLS), F32)
    for t in range(TILTS):
        rows = pltpu.roll(flat_meta[pl.ds(t, NS, stride=4), :], COLS - 2 * BAND + CTRL * t, 1)
        table = jnp.where(lane // CTRL == t, rows, table)
    chosen = dot(jnp.transpose(table)[0:16].astype(BF16), hot16)
    scale = [
        sum(basis[k] * chosen[CTRL * t + k : CTRL * t + k + 1] for k in range(CTRL))
        for t in range(TILTS)
    ]

    other, there = spot("c", 1)
    c_copies, s_x, s_y = [], [], []
    squares = jnp.zeros((NS, COLS), F32)
    for t in range(TILTS):
        total = jnp.sum(jnp.where(hit, scale[t] * scale[t], 0.0), axis=1, keepdims=True)
        squares = jnp.where(lane == t, total, squares)
    bs[:, 0] = squares.reshape(NC * NX, GROUP, COLS)
    slabs = [(0 if t == 0 else 1 + t * BAND, 1 + (t + 1) * BAND) for t in range(TILTS)]
    for t in range(TILTS):
        weight = jnp.where(hit, scale[t], 0.0)
        both = jnp.concatenate(split2(weight), axis=0)
        for u in range(0, BAND, 2):
            r = t * BAND + u
            pair = dot(both, jnp.concatenate([xt[r], xt[r + 1]], axis=1))
            pair = pair[:NS] + pair[NS:]
            bs[:, 1 + r] = pair[:, :COLS].reshape(NC * NX, GROUP, COLS)
            bs[:, 2 + r] = pair[:, COLS:].reshape(NC * NX, GROUP, COLS)
        lo, hi = slabs[t]
        c_copies.append(remote(SC + t, other, bs.at[pl.ds(there * NX, NX), lo:hi], brc.at[:, lo:hi]))
        c_copies[t].start()

    p_z.wait_recv()
    own = psrc[:, z]
    for k in range(1, NZ):
        own = own + prcv[lax.rem(z + k, NZ)]
    pall[c, x, y] = own.reshape(OWN * ROWS, COLS).astype(BF16)
    p_x = send(PX, "x", lambda there: pall.at[c, x, y], pall.at[c, x, y], pall.at[0, 0, 0 : NX - 1])
    p_y = send(PY, "y", lambda there: pall.at[c, x, y], pall.at[c, x, y], pall.at[0, 0, 0 : NY - 1])


    for t in range(TILTS):
        c_copies[t].wait_recv()
        lo, hi = slabs[t]
        brc[:, lo:hi] = brc[:, lo:hi] + bs[pl.ds(c * NX, NX), lo:hi]
        bulk = brx.at[0 : NX - 1, lo:hi]
        s_x.append(
            send(SX + t, "x", lambda there: brc.at[there, lo:hi], brx.at[x, lo:hi], bulk)
        )
    sent += c_copies

    p_x.wait_recv()
    for k in (4, 3, 5, 2, 6, 1, 7):
        for j in range(1, NX):
            block = pall.at[c, lax.rem(x + j, NX), y]
            remote(PXY, spot("y", k)[0], block, block).start()
    bulk = pall.at[0, 0 : NX - 1, 0 : NY - 1]
    p_xy = remote(PXY, other, bulk, bulk)
    sent.append(p_xy)
    p_y.wait_recv()
    pgf[...] = pall[c, x].reshape(GROUP * ROWS, COLS).astype(F32)

    flat_group = meta.at[c, pl.ds(x * NY, NY)].reshape(NY * 8, COLS)
    cells = lax.broadcasted_iota(jnp.int32, (GROUP, CELLS), 1).astype(F32)
    for t in range(TILTS):
        group = flat_group[pl.ds(t, GROUP, stride=4), :]
        for u in range(BAND):
            low = group[:, u : u + 1]
            part = group[:, BAND + u : BAND + u + 1]
            weight = jnp.where(
                cells == low, 1.0 - part, jnp.where(cells == low + BOX, part, 0.0)
            )
            wsp[(t * BAND + u) * GROUP : (t * BAND + u + 1) * GROUP, :] = weight.astype(BF16)

    for t in range(TILTS):
        s_x[t].wait_recv()
        lo, hi = slabs[t]
        total = brc[x, lo:hi]
        for k in range(1, NX):
            total = total + brx[lax.rem(x + k, NX), lo:hi]
        if t == 0:
            squares, total = total[0], total[1:]
        fixed = []
        for u in range(BAND):
            guess = pgf[pl.ds(t * BAND + u, GROUP, stride=ROWS), :]
            fixed.append(total[u] - squares[:, t : t + 1] * guess)
        turned = jnp.transpose(jnp.concatenate(fixed, axis=0))
        ysrc[t] = turned.reshape(NY, CPY, BAND * GROUP).astype(BF16)
        bulk = yrcv.at[t, 0 : NY - 1]
        s_y.append(
            send(SY + t, "y", lambda there: ysrc.at[t, there], yrcv.at[t, y], bulk)
        )

    hot_turned = jnp.transpose(hot).astype(BF16)
    lane_p = lax.broadcasted_iota(jnp.int32, (PARTS, COLS), 1)
    factors = jnp.transpose(jnp.concatenate(scale + basis + [basis[0]], axis=0))
    inner = jnp.zeros((PARTS, COLS), F32)

    p_xy.wait_recv()
    p_c = send(PC, "c", lambda there: pall.at[c], pall.at[c], pall.at[0])
    totals = []
    for t in range(TILTS):
        s_y[t].wait_recv()
        total = ysrc[t, y].astype(F32)
        for k in range(1, NY):
            total = total + yrcv[t, lax.rem(y + k, NY)].astype(F32)
        totals.append(total)
    total = jnp.concatenate(totals, axis=1)
    both = jnp.concatenate(split2(total), axis=0)
    for k in range(NZ):
        part = dot(both, wsp[:, k * SLAB : (k + 1) * SLAB])
        zsrc[k] = (part[:CPY] + part[CPY:]).astype(BF16)
    v_z = send(VZ, "z", lambda there: zsrc.at[there], zrcv.at[z], zrcv.at[0 : NZ - 1])

    p_c.wait_recv()
    pf[...] = pall[...].reshape(NS * ROWS, COLS).astype(F32)
    for t in range(TILTS):
        scale_column = factors[:, t : t + 1]
        acc = jnp.zeros((PARTS, COLS), F32)
        for u in range(0, BAND, 2):
            r = t * BAND + u
            pair = [pf[pl.ds(r + k, NS, stride=ROWS), :].astype(BF16) for k in range(2)]
            guesses = dot(hot_turned, jnp.concatenate(pair, axis=1))
            for k in range(2):
                guess = guesses[:, k * COLS : (k + 1) * COLS]
                left = (xt[r + k].astype(F32) - scale_column * guess).astype(BF16).astype(F32)
                rf[(r + k) * PARTS : (r + k + 1) * PARTS, :] = left
                acc = acc + left * guess
        inner = jnp.where(lane_p // CTRL == t, jnp.sum(acc, axis=1, keepdims=True), inner)

    def narrow(i, _):
        for k in range(16):
            part = rf[pl.ds(i * 16 + k, ROWS, stride=PARTS), :]
            rb[i * 16 + k] = part.reshape(TILTS, BAND, COLS).astype(BF16)
        return 0

    lax.fori_loop(0, PARTS // 16, narrow, 0)
    for k in range(8):
        rows = pl.ds(k * step, step)
        pltpu.make_async_copy(rb.at[rows], res_out.at[rows], lsem.at[7]).start()
    term = jnp.zeros((PARTS, COLS), F32)
    for k in range(CTRL):
        term = jnp.where(lax.rem(lane_p, CTRL) == k, factors[:, TILTS + k : TILTS + k + 1] * inner, term)
    hi, mid, lo = split3(term)
    grad = (dot(hot16, hi) + (dot(hot16, mid) + dot(hot16, lo))) * (-1.0 / (BOX * BOX))
    qsrc[...] = grad.reshape(NC, NX, GROUP, COLS)
    q_c = send(QC, "c", lambda there: qsrc.at[there], qrc, qrc)

    q_c.wait_recv()
    qrc[...] = qrc[...] + qsrc[c]
    q_x = send(QX, "x", lambda there: qrc.at[there], qrx.at[x], qrx.at[0 : NX - 1])
    v_z.wait_recv()
    total = zsrc[z].astype(F32)
    for k in range(1, NZ):
        total = total + zrcv[lax.rem(z + k, NZ)].astype(F32)
    crcv[c] = total
    v_c = send(VC, "c", lambda there: crcv.at[c], crcv.at[c], crcv.at[0])
    v_c.wait_recv()
    xrcv[x] = (crcv[0] + crcv[1]).astype(BF16)
    v_x = send(VX, "x", lambda there: xrcv.at[x], xrcv.at[x], xrcv.at[0 : NX - 1])
    q_x.wait_recv()
    total = qrc[x]
    for k in range(1, NX):
        total = total + qrx[lax.rem(x + k, NX)]
    qry[y] = total
    q_y = send(QY, "y", lambda there: qry.at[y], qry.at[y], qry.at[0 : NY - 1])
    v_x.wait_recv()
    rows = [xrcv[k].astype(F32) for k in range(NX)]
    vall[y] = ((rows[0] + rows[1]) + (rows[2] + rows[3])).astype(BF16)
    v_y = send(VY, "y", lambda there: vall.at[y], vall.at[y], vall.at[0 : NY - 1])
    q_y.wait_recv()
    total = qry[0]
    for k in range(1, NY):
        total = total + qry[k]
    qrz[z] = total
    q_z = send(QZ, "z", lambda there: qrz.at[z], qrz.at[z], qrz.at[0 : NZ - 1])
    q_z.wait_recv()
    total = qrz[0]
    for k in range(1, NZ):
        total = total + qrz[k]
    last[...] = total
    mine = last[pl.ds(y * OWN, OWN), :]
    for t in range(TILTS):
        wg_out[t] = pltpu.roll(mine, (COLS - CTRL * t) % COLS, 1)[:, 0:CTRL]
    v_y.wait_recv()
    back_out[...] = jnp.transpose(vall[...].astype(F32).reshape(COLS, SLAB))
    pltpu.make_async_copy(rb, res_out, lsem.at[7]).wait()
    for copy in sent:
        copy.wait_send()


def hand_over(res_in, grad_in, back_in, res_out, grad_out, back_out, res, grad, back, isem, osem):
    part = PARTS // 8
    ways = [(grad_in, grad, grad_out), (back_in, back, back_out)]
    for k in range(8):
        rows = pl.ds(k * part, part)
        ways.append((res_in.at[rows], res.at[rows], res_out.at[rows]))
    inward = [pltpu.make_async_copy(a, b, isem.at[k]) for k, (a, b, _) in enumerate(ways)]
    outward = [pltpu.make_async_copy(b, c, osem.at[k]) for k, (_, b, c) in enumerate(ways)]
    for copy in inward:
        copy.start()
    for first, second in zip(inward, outward):
        first.wait()
        second.start()
    for copy in outward:
        copy.wait()


def shards(reference_volume, cell_index, cell_frac, warp, series, position, images):
    vmem = pl.BlockSpec(memory_space=pltpu.VMEM)
    hbm = pl.BlockSpec(memory_space=pl.ANY)
    scratch = [
        pltpu.VMEM((SLAB, COLS), BF16),
        pltpu.VMEM((TILTS, OWN, BOX), jnp.int32),
        pltpu.VMEM((TILTS, OWN, BOX), F32),
        pltpu.VMEM((TILTS, OWN, CTRL), BF16),
        pltpu.VMEM((PARTS,), jnp.int32),
        pltpu.VMEM((PARTS,), F32),
        pltpu.VMEM((PARTS, TILTS, BAND, COLS), BF16),
        pltpu.VMEM((PARTS * ROWS, COLS), F32),
        pltpu.VMEM((ROWS, PARTS, COLS), BF16),
        pltpu.VMEM((3, 8, COLS), F32),
        pltpu.VMEM((NC, NX * NY, 8, COLS), F32),
        pltpu.VMEM((OWN * TILTS, NZ, BAND, COLS), F32),
        pltpu.VMEM((NZ, OWN * TILTS, BAND, COLS), F32),
        pltpu.VMEM((NC, NX, NY, OWN * ROWS, COLS), BF16),
        pltpu.VMEM((GROUP * ROWS, COLS), F32),
        pltpu.VMEM((NS * ROWS, COLS), F32),
        pltpu.VMEM((NC * NX, 1 + ROWS, GROUP, COLS), F32),
        pltpu.VMEM((NX, 1 + ROWS, GROUP, COLS), F32),
        pltpu.VMEM((NX, 1 + ROWS, GROUP, COLS), F32),
        pltpu.VMEM((TILTS, NY, CPY, BAND * GROUP), BF16),
        pltpu.VMEM((TILTS, NY, CPY, BAND * GROUP), BF16),
        pltpu.VMEM((ROWS * GROUP, CELLS), BF16),
        pltpu.VMEM((NZ, CPY, SLAB), BF16),
        pltpu.VMEM((NZ, CPY, SLAB), BF16),
        pltpu.VMEM((NC, CPY, SLAB), F32),
        pltpu.VMEM((NX, CPY, SLAB), BF16),
        pltpu.VMEM((NY, CPY, SLAB), BF16),
        pltpu.VMEM((NC, NX, GROUP, COLS), F32),
        pltpu.VMEM((NX, GROUP, COLS), F32),
        pltpu.VMEM((NX, GROUP, COLS), F32),
        pltpu.VMEM((NY, GROUP, COLS), F32),
        pltpu.VMEM((NZ, GROUP, COLS), F32),
        pltpu.VMEM((GROUP, COLS), F32),
        pltpu.VMEM((PARTS * ROWS, COLS), F32),
        pltpu.VMEM((PARTS, TILTS, BAND, COLS), BF16),
        pltpu.SemaphoreType.DMA((EXCHANGES,)),
        pltpu.SemaphoreType.DMA((EXCHANGES,)),
        pltpu.SemaphoreType.DMA((8,)),
    ]
    residual, warp_grad, back_volume = pl.pallas_call(
        kernel,
        out_shape=(
            jax.ShapeDtypeStruct((PARTS, TILTS, BAND, COLS), BF16),
            jax.ShapeDtypeStruct((TILTS, OWN, CTRL), F32),
            jax.ShapeDtypeStruct((SLAB, COLS), F32),
        ),
        in_specs=[hbm] * 7,
        out_specs=(hbm, vmem, vmem),
        scratch_shapes=scratch,
        compiler_params=pltpu.CompilerParams(
            collective_id=0, has_side_effects=True, vmem_limit_bytes=56 << 20
        ),
        name="refine",
    )(
        reference_volume,
        jnp.transpose(cell_index, (1, 0, 2)),
        jnp.transpose(cell_frac, (1, 0, 2)),
        jnp.transpose(warp, (2, 1, 0)),
        series,
        position,
        images,
    )
    residual, warp_grad, back_volume = pl.pallas_call(
        hand_over,
        out_shape=(
            jax.ShapeDtypeStruct(residual.shape, BF16),
            jax.ShapeDtypeStruct(warp_grad.shape, F32),
            jax.ShapeDtypeStruct(back_volume.shape, F32),
        ),
        in_specs=[hbm] * 3,
        out_specs=(hbm, hbm, hbm),
        scratch_shapes=[
            pltpu.VMEM(residual.shape, BF16),
            pltpu.VMEM(warp_grad.shape, F32),
            pltpu.VMEM(back_volume.shape, F32),
            pltpu.SemaphoreType.DMA((10,)),
            pltpu.SemaphoreType.DMA((10,)),
        ],
        name="hand_over",
    )(residual, warp_grad, back_volume)
    return residual, jnp.transpose(warp_grad, (2, 1, 0)), back_volume


def solution(mesh):
    placed = (
        P("slab", None),
        P("dom", None, None),
        P("dom", None, None),
        P(None, "dom", None),
        P("dom"),
        P("dom"),
        P("dom", None, "slab", None),
    )
    return jax.shard_map(
        shards,
        mesh=mesh,
        in_specs=placed,
        out_specs=(P("dom", None, "slab", None), P(None, "dom", None), P("slab", None)),
        check_vma=False,
    )
```

```python
import jax
import jax.numpy as jnp
from jax import lax
from jax.experimental import pallas as pl
from jax.experimental.pallas import tpu as pltpu
from jax.sharding import PartitionSpec as P

MESH = pl.DeviceIdType.MESH
F32, BF16 = jnp.float32, jnp.bfloat16
NY, NX, NC, NZ = 8, 4, 2, 8
BOX, TILTS, CTRL, COLS = 64, 3, 4, 128
PARTS = 256
BAND = BOX // NZ
ROWS = TILTS * BAND
OWN = 2
NS = NY * NX * NC * OWN
GROUP = NY * OWN
SLAB = BOX * BOX // NZ
CELLS = BOX * BOX
CPY = COLS // NY

(META_Y, META_X, META_C, PZ, PY, PX, PC, VZ, VC, VX, VY, QC, QX, QY, QZ, PXY) = range(16)
SC, SX, SY, EXCHANGES = 16, 16 + TILTS, 16 + 2 * TILTS, 16 + 3 * TILTS


def split2(v):
    hi = v.astype(BF16)
    return hi, (v - hi.astype(F32)).astype(BF16)


def split3(v):
    hi = v.astype(BF16)
    rest = v - hi.astype(F32)
    mid = rest.astype(BF16)
    return hi, mid, (rest - mid.astype(F32)).astype(BF16)


def dot(a, b):
    return jnp.dot(a, b, preferred_element_type=F32)


def kernel(
    vol_in,
    idx_in,
    frac_in,
    warp_in,
    series_in,
    pos_in,
    images,
    res_out,
    wg_out,
    back_out,
    vol,
    idx,
    frac,
    warp,
    series,
    pos,
    imgv,
    xf,
    xt,
    tmp,
    meta,
    psrc,
    prcv,
    pall,
    pgf,
    pf,
    bs,
    brc,
    brx,
    ysrc,
    yrcv,
    wsp,
    zsrc,
    zrcv,
    xrcv,
    vall,
    qsrc,
    qrx,
    qry,
    qrz,
    last,
    rf,
    rb,
    ssem,
    rsem,
    lsem,
):
    d, z = lax.axis_index("dom"), lax.axis_index("slab")
    c, x, y = lax.rem(d, NC), lax.rem(d // NC, NX), d // (NC * NX)

    def spot(axis, k):
        at = {"y": y, "x": x, "c": c, "z": z}
        size = {"y": NY, "x": NX, "c": NC, "z": NZ}[axis]
        at[axis] = lax.rem(at[axis] + k, size)
        return ((at["y"] * NX + at["x"]) * NC + at["c"], at["z"]), at[axis]

    def remote(row, device, src, dst):
        return pltpu.make_async_remote_copy(
            src_ref=src,
            dst_ref=dst,
            send_sem=ssem.at[row],
            recv_sem=rsem.at[row],
            device_id=device,
            device_id_type=MESH,
        )

    def send(row, axis, src, dst, bulk):
        size = {"y": NY, "x": NX, "c": NC, "z": NZ}[axis]
        for k in sorted(range(1, size), key=lambda k: -min(k, size - k)):
            device, there = spot(axis, k)
            remote(row, device, src(there), dst).start()
        whole = remote(row, spot(axis, 1)[0], bulk, bulk)
        sent.append(whole)
        return whole

    def send_group(row, src, dst, bulk):
        for k in (2, 6, 1, 3, 5, 7, 4):
            xx, cc = lax.rem(x + k % NX, NX), lax.rem(c + k // NX, NC)
            remote(row, ((y * NX + xx) * NC + cc, z), src(cc, xx), dst).start()
        whole = remote(row, spot("c", 1)[0], bulk, bulk)
        sent.append(whole)
        return whole

    sent = []

    barrier = pltpu.get_barrier_semaphore()
    partners = [spot("z", k)[0] for k in range(1, NZ)]
    partners += [((y * NX + lax.rem(x + k, NX)) * NC + 1 - c, z) for k in range(NX)]
    plane = []
    steps = [min(j // NX, NY - j // NX) + min(j % NX, NX - j % NX) for j in range(NY * NX)]
    for j in sorted(range(1, NY * NX), key=lambda j: -steps[j]):
        there = lax.rem(y + j // NX, NY) * NX + lax.rem(x + j % NX, NX)
        plane.append((there * NC + c, z))
    for device in plane + partners:
        pl.semaphore_signal(barrier, inc=1, device_id=device, device_id_type=MESH)

    small_copies = [
        pltpu.make_async_copy(a, b, lsem.at[k])
        for k, (a, b) in enumerate(
            (
                (idx_in, idx),
                (frac_in, frac),
                (warp_in, warp),
                (vol_in, vol),
                (series_in, series),
                (pos_in, pos),
            )
        )
    ]
    for copy in small_copies:
        copy.start()
    step = PARTS // 8
    for k in range(8):
        rows = pl.ds(k * step, step)
        pltpu.make_async_copy(images.at[rows], imgv.at[rows], lsem.at[6]).start()

    lane8 = lax.broadcasted_iota(jnp.int32, (8, COLS), 1)
    tmp[...] = jnp.zeros_like(tmp)
    for copy in small_copies[:3]:
        copy.wait()
    for q in range(OWN):
        for t in range(TILTS):
            at = q * 4 + t
            tmp[0, at : at + 1, 0:BOX] = idx[t, q : q + 1].astype(F32)
            tmp[1, at : at + 1, 0:BOX] = frac[t, q : q + 1]
            tmp[2, at : at + 1, 0:CTRL] = warp[t].astype(F32)[q : q + 1]
    own_idx, own_frac, own_warp = tmp[0], tmp[1], tmp[2]
    band_idx = pltpu.roll(own_idx, lax.rem(COLS - z * BAND, COLS), 1)
    band_frac = pltpu.roll(own_frac, lax.rem(COLS - z * BAND + BAND, COLS), 1)
    rolled_warp = pltpu.roll(own_warp, 2 * BAND, 1)
    own_at = x * NY + y
    meta[c, own_at] = jnp.where(
        lane8 < BAND, band_idx, jnp.where(lane8 < 2 * BAND, band_frac, rolled_warp)
    )

    pl.semaphore_wait(barrier, len(partners + plane))
    for device in plane:
        remote(META_Y, device, meta.at[c, own_at], meta.at[c, own_at]).start()
    meta_p = remote(META_Y, plane[0], meta.at[0, 1:], meta.at[0, 1:])
    sent.append(meta_p)

    columns = jnp.transpose(jnp.where(lane8 < BOX, own_idx, pltpu.roll(own_frac, BOX, 1)))
    cell = (lax.broadcasted_iota(jnp.int32, (BOX, SLAB), 1) + z * SLAB).astype(F32)
    small_copies[3].wait()
    volume = vol[...]
    for q in range(OWN):
        for t in range(TILTS):
            low = columns[0:BOX, q * 4 + t : q * 4 + t + 1]
            part = columns[BOX : 2 * BOX, q * 4 + t : q * 4 + t + 1]
            weight = jnp.where(cell == low, 1.0 - part, 0.0) + jnp.where(cell == low + BOX, part, 0.0)
            hi, mid, lo = split3(weight)
            value = dot(hi, volume) + (dot(mid, volume) + dot(lo, volume))
            psrc[q * TILTS + t] = value.reshape(NZ, BAND, COLS)

    p_z = send(PZ, "z", lambda there: psrc.at[:, there], prcv.at[z], prcv.at[0 : NZ - 1])

    pltpu.make_async_copy(images, imgv, lsem.at[6]).wait()
    for copy in small_copies[4:]:
        copy.wait()

    def widen(i, _):
        part = imgv[pl.ds(i * 32, 32)].astype(F32)
        xf[pl.ds(pl.multiple_of(i * 32 * ROWS, 32 * ROWS), 32 * ROWS), :] = part.reshape(32 * ROWS, COLS)
        return 0

    lax.fori_loop(0, PARTS // 32, widen, 0)

    def gather_rows(r, _):
        xt[r] = xf[pl.ds(r, PARTS, stride=ROWS), :].astype(BF16)
        return 0

    lax.fori_loop(0, ROWS, gather_rows, 0)

    row = lax.broadcasted_iota(jnp.int32, (NS, PARTS), 0)
    name = (
        lax.rem(row, GROUP) // OWN * (NX * NC * OWN)
        + lax.rem(row // GROUP, NX) * (NC * OWN)
        + row // (GROUP * NX) * OWN
        + lax.rem(row, OWN)
    )
    hit = series[...].reshape(1, PARTS) == name
    hot = hit.astype(F32)
    hot16 = hot.astype(BF16)
    at = pos[...].reshape(1, PARTS)
    remain = 1.0 - at
    square = at * at
    cubed = square * at
    basis = [
        remain * remain * remain / 6.0,
        (3.0 * cubed - 6.0 * square + 4.0) / 6.0,
        (-3.0 * cubed + 3.0 * square + 3.0 * at + 1.0) / 6.0,
        cubed / 6.0,
    ]

    meta_p.wait_recv()
    meta_c = send(META_C, "c", lambda there: meta.at[c], meta.at[c], meta.at[0])
    meta_c.wait_recv()

    flat_meta = meta.reshape(NS * 4, COLS)
    lane = lax.broadcasted_iota(jnp.int32, (NS, COLS), 1)
    table = jnp.zeros((NS, COLS), F32)
    for t in range(TILTS):
        rows = pltpu.roll(flat_meta[pl.ds(t, NS, stride=4), :], COLS - 2 * BAND + CTRL * t, 1)
        table = jnp.where(lane // CTRL == t, rows, table)
    chosen = dot(jnp.transpose(table)[0:16].astype(BF16), hot16)
    scale = [
        sum(basis[k] * chosen[CTRL * t + k : CTRL * t + k + 1] for k in range(CTRL))
        for t in range(TILTS)
    ]

    other, there = spot("c", 1)
    c_copies, s_x, s_y = [], [], []
    squares = jnp.zeros((NS, COLS), F32)
    for t in range(TILTS):
        total = jnp.sum(jnp.where(hit, scale[t] * scale[t], 0.0), axis=1, keepdims=True)
        squares = jnp.where(lane == t, total, squares)
    bs[:, 0] = squares.reshape(NC * NX, GROUP, COLS)
    slabs = [(0 if t == 0 else 1 + t * BAND, 1 + (t + 1) * BAND) for t in range(TILTS)]
    for t in range(TILTS):
        weight = jnp.where(hit, scale[t], 0.0)
        both = jnp.concatenate(split2(weight), axis=0)
        for u in range(0, BAND, 2):
            r = t * BAND + u
            pair = dot(both, jnp.concatenate([xt[r], xt[r + 1]], axis=1))
            pair = pair[:NS] + pair[NS:]
            bs[:, 1 + r] = pair[:, :COLS].reshape(NC * NX, GROUP, COLS)
            bs[:, 2 + r] = pair[:, COLS:].reshape(NC * NX, GROUP, COLS)
        lo, hi = slabs[t]
        c_copies.append(remote(SC + t, other, bs.at[pl.ds(there * NX, NX), lo:hi], brc.at[:, lo:hi]))
        c_copies[t].start()

    p_z.wait_recv()
    own = psrc[:, z]
    for k in range(1, NZ):
        own = own + prcv[lax.rem(z + k, NZ)]
    pall[c, x, y] = own.reshape(OWN * ROWS, COLS).astype(BF16)
    p_x = send(PX, "x", lambda there: pall.at[c, x, y], pall.at[c, x, y], pall.at[0, 0, 0 : NX - 1])
    p_y = send(PY, "y", lambda there: pall.at[c, x, y], pall.at[c, x, y], pall.at[0, 0, 0 : NY - 1])


    for t in range(TILTS):
        c_copies[t].wait_recv()
        lo, hi = slabs[t]
        brc[:, lo:hi] = brc[:, lo:hi] + bs[pl.ds(c * NX, NX), lo:hi]
        bulk = brx.at[0 : NX - 1, lo:hi]
        s_x.append(
            send(SX + t, "x", lambda there: brc.at[there, lo:hi], brx.at[x, lo:hi], bulk)
        )
    sent += c_copies

    p_x.wait_recv()
    for k in (4, 3, 5, 2, 6, 1, 7):
        for j in range(1, NX):
            block = pall.at[c, lax.rem(x + j, NX), y]
            remote(PXY, spot("y", k)[0], block, block).start()
    bulk = pall.at[0, 0 : NX - 1, 0 : NY - 1]
    p_xy = remote(PXY, other, bulk, bulk)
    sent.append(p_xy)
    p_y.wait_recv()
    pgf[...] = pall[c, x].reshape(GROUP * ROWS, COLS).astype(F32)

    flat_group = meta.at[c, pl.ds(x * NY, NY)].reshape(NY * 8, COLS)
    cells = lax.broadcasted_iota(jnp.int32, (GROUP, CELLS), 1).astype(F32)
    for t in range(TILTS):
        group = flat_group[pl.ds(t, GROUP, stride=4), :]
        for u in range(BAND):
            low = group[:, u : u + 1]
            part = group[:, BAND + u : BAND + u + 1]
            weight = jnp.where(
                cells == low, 1.0 - part, jnp.where(cells == low + BOX, part, 0.0)
            )
            wsp[(t * BAND + u) * GROUP : (t * BAND + u + 1) * GROUP, :] = weight.astype(BF16)

    for t in range(TILTS):
        s_x[t].wait_recv()
        lo, hi = slabs[t]
        total = brc[x, lo:hi]
        for k in range(1, NX):
            total = total + brx[lax.rem(x + k, NX), lo:hi]
        if t == 0:
            squares, total = total[0], total[1:]
        fixed = []
        for u in range(BAND):
            guess = pgf[pl.ds(t * BAND + u, GROUP, stride=ROWS), :]
            fixed.append(total[u] - squares[:, t : t + 1] * guess)
        turned = jnp.transpose(jnp.concatenate(fixed, axis=0))
        ysrc[t] = turned.reshape(NY, CPY, BAND * GROUP).astype(BF16)
        bulk = yrcv.at[t, 0 : NY - 1]
        s_y.append(
            send(SY + t, "y", lambda there: ysrc.at[t, there], yrcv.at[t, y], bulk)
        )

    hot_turned = jnp.transpose(hot).astype(BF16)
    lane_p = lax.broadcasted_iota(jnp.int32, (PARTS, COLS), 1)
    factors = jnp.transpose(jnp.concatenate(scale + basis + [basis[0]], axis=0))
    inner = jnp.zeros((PARTS, COLS), F32)

    p_xy.wait_recv()
    p_c = send(PC, "c", lambda there: pall.at[c], pall.at[c], pall.at[0])
    totals = []
    for t in range(TILTS):
        s_y[t].wait_recv()
        total = ysrc[t, y].astype(F32)
        for k in range(1, NY):
            total = total + yrcv[t, lax.rem(y + k, NY)].astype(F32)
        totals.append(total)
    total = jnp.concatenate(totals, axis=1)
    both = jnp.concatenate(split2(total), axis=0)
    for k in (4, 3, 5, 2, 6, 1, 7, 0):
        device, at = spot("z", k)
        part = dot(both, wsp[:, pl.ds(pl.multiple_of(at * SLAB, SLAB), SLAB)])
        zsrc[at] = (part[:CPY] + part[CPY:]).astype(BF16)
        if k > 0:
            remote(VZ, device, zsrc.at[at], zrcv.at[z]).start()
    v_z = remote(VZ, other, zrcv.at[1:], zrcv.at[1:])
    sent.append(v_z)

    p_c.wait_recv()
    pf[...] = pall[...].reshape(NS * ROWS, COLS).astype(F32)
    for t in range(TILTS):
        scale_column = factors[:, t : t + 1]
        acc = jnp.zeros((PARTS, COLS), F32)
        for u in range(0, BAND, 2):
            r = t * BAND + u
            pair = [pf[pl.ds(r + k, NS, stride=ROWS), :].astype(BF16) for k in range(2)]
            guesses = dot(hot_turned, jnp.concatenate(pair, axis=1))
            for k in range(2):
                guess = guesses[:, k * COLS : (k + 1) * COLS]
                left = (xt[r + k].astype(F32) - scale_column * guess).astype(BF16).astype(F32)
                rf[(r + k) * PARTS : (r + k + 1) * PARTS, :] = left
                acc = acc + left * guess
        inner = jnp.where(lane_p // CTRL == t, jnp.sum(acc, axis=1, keepdims=True), inner)

    term = jnp.zeros((PARTS, COLS), F32)
    for k in range(CTRL):
        term = jnp.where(lax.rem(lane_p, CTRL) == k, factors[:, TILTS + k : TILTS + k + 1] * inner, term)
    hi, mid, lo = split3(term)
    grad = (dot(hot16, hi) + (dot(hot16, mid) + dot(hot16, lo))) * (-1.0 / (BOX * BOX))
    qsrc[...] = grad.reshape(NC, NX, GROUP, COLS)
    q_x = send_group(QX, lambda cc, xx: qsrc.at[cc, xx], qrx.at[c * NX + x], qrx.at[1:])

    def narrow(i, _):
        for k in range(16):
            part = rf[pl.ds(i * 16 + k, ROWS, stride=PARTS), :]
            rb[i * 16 + k] = part.reshape(TILTS, BAND, COLS).astype(BF16)
        return 0

    lax.fori_loop(0, PARTS // 16, narrow, 0)
    for k in range(8):
        rows = pl.ds(k * step, step)
        pltpu.make_async_copy(rb.at[rows], res_out.at[rows], lsem.at[7]).start()
    v_z.wait_recv()
    total = zsrc[z].astype(F32)
    for k in range(1, NZ):
        total = total + zrcv[lax.rem(z + k, NZ)].astype(F32)
    at_group = c * NX + x
    xrcv[at_group] = total.astype(BF16)
    v_x = send_group(VX, lambda cc, xx: xrcv.at[at_group], xrcv.at[at_group], xrcv.at[1:])
    q_x.wait_recv()
    total = qsrc[c, x]
    for k in range(1, NC * NX):
        total = total + qrx[lax.rem(c + k // NX, NC) * NX + lax.rem(x + k, NX)]
    qry[y] = total
    q_y = send(QY, "y", lambda there: qry.at[y], qry.at[y], qry.at[0 : NY - 1])
    v_x.wait_recv()
    total = xrcv[0].astype(F32)
    for k in range(1, NC * NX):
        total = total + xrcv[k].astype(F32)
    vall[y] = total.astype(BF16)
    v_y = send(VY, "y", lambda there: vall.at[y], vall.at[y], vall.at[0 : NY - 1])
    q_y.wait_recv()
    total = qry[0]
    for k in range(1, NY):
        total = total + qry[k]
    qrz[z] = total
    q_z = send(QZ, "z", lambda there: qrz.at[z], qrz.at[z], qrz.at[0 : NZ - 1])
    q_z.wait_recv()
    total = qrz[0]
    for k in range(1, NZ):
        total = total + qrz[k]
    last[...] = total
    mine = last[pl.ds(y * OWN, OWN), :]
    for t in range(TILTS):
        wg_out[t] = pltpu.roll(mine, (COLS - CTRL * t) % COLS, 1)[:, 0:CTRL]
    v_y.wait_recv()
    back_out[...] = jnp.transpose(vall[...].astype(F32).reshape(COLS, SLAB))
    pltpu.make_async_copy(rb, res_out, lsem.at[7]).wait()
    for copy in sent:
        copy.wait_send()


def hand_over(res_in, grad_in, back_in, res_out, grad_out, back_out, res, grad, back, isem, osem):
    part = PARTS // 8
    ways = [(grad_in, grad, grad_out), (back_in, back, back_out)]
    for k in range(8):
        rows = pl.ds(k * part, part)
        ways.append((res_in.at[rows], res.at[rows], res_out.at[rows]))
    inward = [pltpu.make_async_copy(a, b, isem.at[k]) for k, (a, b, _) in enumerate(ways)]
    outward = [pltpu.make_async_copy(b, c, osem.at[k]) for k, (_, b, c) in enumerate(ways)]
    for copy in inward:
        copy.start()
    for first, second in zip(inward, outward):
        first.wait()
        second.start()
    for copy in outward:
        copy.wait()


def shards(reference_volume, cell_index, cell_frac, warp, series, position, images):
    vmem = pl.BlockSpec(memory_space=pltpu.VMEM)
    hbm = pl.BlockSpec(memory_space=pl.ANY)
    scratch = [
        pltpu.VMEM((SLAB, COLS), BF16),
        pltpu.VMEM((TILTS, OWN, BOX), jnp.int32),
        pltpu.VMEM((TILTS, OWN, BOX), F32),
        pltpu.VMEM((TILTS, OWN, CTRL), BF16),
        pltpu.VMEM((PARTS,), jnp.int32),
        pltpu.VMEM((PARTS,), F32),
        pltpu.VMEM((PARTS, TILTS, BAND, COLS), BF16),
        pltpu.VMEM((PARTS * ROWS, COLS), F32),
        pltpu.VMEM((ROWS, PARTS, COLS), BF16),
        pltpu.VMEM((3, 8, COLS), F32),
        pltpu.VMEM((NC, NX * NY, 8, COLS), F32),
        pltpu.VMEM((OWN * TILTS, NZ, BAND, COLS), F32),
        pltpu.VMEM((NZ, OWN * TILTS, BAND, COLS), F32),
        pltpu.VMEM((NC, NX, NY, OWN * ROWS, COLS), BF16),
        pltpu.VMEM((GROUP * ROWS, COLS), F32),
        pltpu.VMEM((NS * ROWS, COLS), F32),
        pltpu.VMEM((NC * NX, 1 + ROWS, GROUP, COLS), F32),
        pltpu.VMEM((NX, 1 + ROWS, GROUP, COLS), F32),
        pltpu.VMEM((NX, 1 + ROWS, GROUP, COLS), F32),
        pltpu.VMEM((TILTS, NY, CPY, BAND * GROUP), BF16),
        pltpu.VMEM((TILTS, NY, CPY, BAND * GROUP), BF16),
        pltpu.VMEM((ROWS * GROUP, CELLS), BF16),
        pltpu.VMEM((NZ, CPY, SLAB), BF16),
        pltpu.VMEM((NZ, CPY, SLAB), BF16),
        pltpu.VMEM((NC * NX, CPY, SLAB), BF16),
        pltpu.VMEM((NY, CPY, SLAB), BF16),
        pltpu.VMEM((NC, NX, GROUP, COLS), F32),
        pltpu.VMEM((NC * NX, GROUP, COLS), F32),
        pltpu.VMEM((NY, GROUP, COLS), F32),
        pltpu.VMEM((NZ, GROUP, COLS), F32),
        pltpu.VMEM((GROUP, COLS), F32),
        pltpu.VMEM((PARTS * ROWS, COLS), F32),
        pltpu.VMEM((PARTS, TILTS, BAND, COLS), BF16),
        pltpu.SemaphoreType.DMA((EXCHANGES,)),
        pltpu.SemaphoreType.DMA((EXCHANGES,)),
        pltpu.SemaphoreType.DMA((8,)),
    ]
    residual, warp_grad, back_volume = pl.pallas_call(
        kernel,
        out_shape=(
            jax.ShapeDtypeStruct((PARTS, TILTS, BAND, COLS), BF16),
            jax.ShapeDtypeStruct((TILTS, OWN, CTRL), F32),
            jax.ShapeDtypeStruct((SLAB, COLS), F32),
        ),
        in_specs=[hbm] * 7,
        out_specs=(hbm, vmem, vmem),
        scratch_shapes=scratch,
        compiler_params=pltpu.CompilerParams(
            collective_id=0, has_side_effects=True, vmem_limit_bytes=56 << 20
        ),
        name="refine",
    )(
        reference_volume,
        jnp.transpose(cell_index, (1, 0, 2)),
        jnp.transpose(cell_frac, (1, 0, 2)),
        jnp.transpose(warp, (2, 1, 0)),
        series,
        position,
        images,
    )
    residual, warp_grad, back_volume = pl.pallas_call(
        hand_over,
        out_shape=(
            jax.ShapeDtypeStruct(residual.shape, BF16),
            jax.ShapeDtypeStruct(warp_grad.shape, F32),
            jax.ShapeDtypeStruct(back_volume.shape, F32),
        ),
        in_specs=[hbm] * 3,
        out_specs=(hbm, hbm, hbm),
        scratch_shapes=[
            pltpu.VMEM(residual.shape, BF16),
            pltpu.VMEM(warp_grad.shape, F32),
            pltpu.VMEM(back_volume.shape, F32),
            pltpu.SemaphoreType.DMA((10,)),
            pltpu.SemaphoreType.DMA((10,)),
        ],
        name="hand_over",
    )(residual, warp_grad, back_volume)
    return residual, jnp.transpose(warp_grad, (2, 1, 0)), back_volume


def solution(mesh):
    placed = (
        P("slab", None),
        P("dom", None, None),
        P("dom", None, None),
        P(None, "dom", None),
        P("dom"),
        P("dom"),
        P("dom", None, "slab", None),
    )
    return jax.shard_map(
        shards,
        mesh=mesh,
        in_specs=placed,
        out_specs=(P("dom", None, "slab", None), P(None, "dom", None), P("slab", None)),
        check_vma=False,
    )
```
